32 devices in a mesh: blk: 8 (over y, x, core), exp: 4 (over z).
Axes of the slice: x: 2, y: 2, z: 4, core: 2. Of those that a mesh axis runs over, the one named last changes fastest.
Arguments:
- hidden: bfloat16 [1024, 2560], P('exp', 'blk'), may hold values from -6 to 6
- attn_gain: float32 [2560], replicated, may hold values from 0.25 to 1.75
- qkv_weight: bfloat16 [2560, 3584], P(None, 'blk'), may hold values from -0.125 to 0.125
- out_weight: bfloat16 [2560, 2560], P(None, 'blk'), may hold values from -0.125 to 0.125
- kv_pool: bfloat16 [4, 32, 128, 1024], P('exp', 'blk'), may hold values from -64 to 64
- page_table: int32 [4, 32], P('exp'), may hold values from 0 to 31, each once within a row
- cache_lens: int32 [4], P('exp'), may hold values from 1 to 3840, as said below
- ffn_gain: float32 [2560], replicated, may hold values from 0.25 to 1.75
- route_ids: int32 [1024, 6], P('exp'), may hold values from 0 to 7, all different within a row; in each aligned block of 256 rows (0 to 255, 256 to 511, ...) at most 256 rows name the same one
- route_weights: float32 [1024, 6], P('exp'), may hold values from 0.05 to 2
- shared_gate_up: bfloat16 [2560, 2, 3072], P(None, None, 'blk'), may hold values from -0.125 to 0.125
- shared_down: bfloat16 [3072, 2560], P('blk'), may hold values from -0.109375 to 0.109375
- expert_gate_up: bfloat16 [32, 2560, 768], P(('blk', 'exp')), may hold values from -0.125 to 0.125
- expert_down: bfloat16 [32, 384, 2560], P(('blk', 'exp')), may hold values from -0.3125 to 0.3125
Outputs:
- hidden_out: bfloat16 [1024, 2560], P('exp', 'blk')
- kv_pool_out: bfloat16 [4, 32, 128, 1024], P('exp', 'blk')
The draws below stay inside these ranges and needn't reach their ends.
Inputs may be any that keep to these rules, and one draw needn't show every extreme that they name: `route_ids`: among the 256 tokens of one request at most 256 choose any one expert, and some expert is chosen by exactly 256 of them; a token's 6 experts differ. `page_table`: each row names every page of the request's pool once. `cache_lens`: some request has exactly 3840 cached tokens.
All inputs are finite; a program needn't handle non-finite values.
Results may differ from the reference program's by a relative error of at most 0.02.
The reference program's roundings to bfloat16 on the way count: a program that leaves them out, or rounds other values in their place, can miss the bound.
Values may be sent and summed in bfloat16 or wider, within the bound.
A program may use at most 256 MiB of HBM per device.

```python
import math
import jax
import jax.numpy as jnp
import numpy as np
from jax import lax

D = 2560
HEADS = 20
KV_HEADS = 4
HEAD_DIM = 128
TOPK = 6
FF_SHARED = 3072
SPLIT = 4
PAGE = 128
NEW = 256
EXPERTS = 8
REQUESTS = 4
TOKENS = 1024
POOL = 32
CMAX = 3840
CAP = 256
QKV_W = 3584
FF_PART = 384
N_EXP = 4


def draw_cache_lens(key, part):
    first_key, second_key = jax.random.split(key)
    lengths = jax.random.randint(first_key, (REQUESTS,), 1, CMAX + 1)
    longest = jax.random.randint(second_key, (), 0, REQUESTS)
    return jnp.where(jnp.arange(REQUESTS) == longest, CMAX, lengths).astype(jnp.int32)


def draw_kv_pool(key, part):
    shape = (REQUESTS, POOL, PAGE, 2 * KV_HEADS * HEAD_DIM)
    first_key = jax.random.fold_in(jax.random.fold_in(key, 11), 0)
    values = jax.random.normal(first_key, shape, jnp.float32)
    return jnp.clip(values, -64.0, 64.0).astype(jnp.bfloat16)


def level_of(rng, dims, pieces, least, high):
    gain = 1.0
    for dim, parts in pieces:
        draws = jax.random.uniform(jax.random.fold_in(jax.random.fold_in(rng, 6), dim), (parts,), jnp.float32, least / len(pieces), high / len(pieces))
        gain = gain * jnp.repeat(jnp.exp(draws), dims[dim] // parts).reshape((-1,) + (1,) * (len(dims) - 1 - dim))
    return gain


def assign_block(key, own, number, rows, count, top, bound, lean):
    order = jax.random.permutation(key, count)
    heavy_load, usual = portions_of(count, rows * top, bound, lean, True), portions_of(count, rows * top, bound, lean, False)
    places = jnp.arange(count)

    def named(tallies, offset_by):
        used = int((tallies > 0).sum())
        fixed = max(1, used // 4)
        passed = fixed + (places - fixed + offset_by * (used - fixed)) % max(1, count - fixed)
        return jnp.zeros((count,), jnp.int32).at[order[jnp.where(places < fixed, places, passed)]].set(jnp.asarray(tallies, jnp.int32))

    tallies = jnp.where(number % 4 == 0, named(heavy_load, number // 4), named(usual, number - number // 4 - 1))
    mixed = jax.random.permutation(jax.random.fold_in(own, 3), count)
    giver, sink = mixed[0:count // 2 * 2:2], mixed[1:count // 2 * 2:2]
    slack = jnp.minimum(tallies[giver] - 1, bound - tallies[sink]) // 2
    slack = jnp.where((giver == order[0]) | (sink == order[0]) | (tallies[sink] == 0), 0, jnp.maximum(slack, 0))
    passed = jax.random.randint(jax.random.fold_in(own, 4), (count // 2,), 0, 1 << 20) % (slack + 1)
    tallies = tallies.at[giver].add(-passed).at[sink].add(passed)
    labels = jnp.searchsorted(jnp.cumsum(tallies), jnp.arange(rows * top), side="right").astype(jnp.int32)
    grid = labels.reshape(top, rows).T
    grid = grid[jax.random.permutation(jax.random.fold_in(own, 1), rows)]
    offset_by = jax.random.randint(jax.random.fold_in(own, 2), (rows, 1), 0, top)
    return jnp.take_along_axis(grid, (jnp.arange(top)[None, :] + offset_by) % top, axis=1)


def portions_of(number_of, total, reach, slope, full):
    portions = [(1 << 20) // math.isqrt(rank ** slope) + 1 for rank in range(1, number_of + 1)]
    largest = reach if full else min(reach, max(-(-total // number_of), total * portions[0] // sum(portions)))
    least = 1 if total - largest >= number_of - 1 else 0
    counts, surplus = [largest] + [least] * (number_of - 1), total - largest - least * (number_of - 1)
    while surplus > 0:
        free = [i for i in range(1, number_of) if counts[i] < largest] or [i for i in range(1, number_of) if counts[i] < reach]
        whole, budget = sum([portions[i] for i in free]), surplus
        for i in free:
            addition = min(reach - counts[i], max(1, budget * portions[i] // whole), surplus)
            counts[i] = counts[i] + addition
            surplus = surplus - addition
    return np.array(counts)


def centred(rng, extent, spread, reach, cuts=(), dtype=jnp.bfloat16):
    values = spread * jax.random.normal(rng, extent, jnp.float32)
    if cuts:
        values = values * level_of(rng, extent, cuts, -0.22, 0.18)
    return jnp.clip(values, -reach, reach).astype(dtype)


def setup_inputs(seed: int = 0) -> dict:
    splits = jax.random.split(jax.random.key(seed), 15)
    hidden = centred(splits[0], (TOKENS, D), 1.0, 6.0, ((0, 4), (1, 8)))
    attn_gain = jnp.clip(1.0 + 0.15 * jax.random.normal(splits[1], (D,), jnp.float32), 0.25, 1.75)
    qkv_weight = centred(splits[2], (D, QKV_W), D ** -0.5, 0.125, ((1, 8),))
    out_weight = centred(splits[3], (D, D), D ** -0.5, 0.125, ((1, 8),))
    kv_pool = draw_kv_pool(jax.random.fold_in(splits[14], 71), 0)
    page_table = jax.vmap(lambda own: jax.random.permutation(own, POOL))(jax.random.split(splits[5], REQUESTS)).reshape((REQUESTS, POOL)).astype(jnp.int32)
    cache_lens = draw_cache_lens(jax.random.fold_in(splits[14], 71), 0)
    ffn_gain = jnp.clip(1.0 + 0.15 * jax.random.normal(splits[7], (D,), jnp.float32), 0.25, 1.75)
    route_ids_keys = jax.random.split(jax.random.fold_in(splits[8], 1), TOKENS // NEW)
    route_ids_turns = jax.random.permutation(jax.random.fold_in(splits[8], 3), TOKENS // NEW)
    route_ids = jax.vmap(lambda own, number: assign_block(jax.random.fold_in(splits[8], 2), own, number, NEW, EXPERTS, TOPK, CAP, 1))(route_ids_keys, route_ids_turns).reshape((TOKENS, TOPK))
    route_weights = jnp.clip(jnp.exp(math.log(2.0) - 3.6888794 * jax.random.uniform(splits[9], (TOKENS, TOPK), jnp.float32) ** level_of(splits[9], (TOKENS, TOPK), ((0, 4),), -0.2, 0.2)), 0.05, 2.0)
    shared_gate_up = centred(splits[10], (D, 2, FF_SHARED), D ** -0.5, 0.125, ((2, 8),))
    shared_down = centred(splits[11], (FF_SHARED, D), FF_SHARED ** -0.5, 0.109375, ((0, 8),))
    expert_gate_up = centred(splits[12], (EXPERTS * SPLIT, D, 2 * FF_PART), D ** -0.5, 0.125, ((0, 32),))
    expert_down = centred(splits[13], (EXPERTS * SPLIT, FF_PART, D), FF_PART ** -0.5, 0.3125, ((0, 32),))
    return dict(hidden=hidden, attn_gain=attn_gain, qkv_weight=qkv_weight, out_weight=out_weight, kv_pool=kv_pool, page_table=page_table, cache_lens=cache_lens, ffn_gain=ffn_gain, route_ids=route_ids, route_weights=route_weights, shared_gate_up=shared_gate_up, shared_down=shared_down, expert_gate_up=expert_gate_up, expert_down=expert_down)


rope_base = 500000.0
norm_eps = 1e-05

def normalize(inputs, gain_vec):
    values = inputs.astype(jnp.float32)
    inv_rms = lax.rsqrt(lax.optimization_barrier(jnp.mean(values * values, axis=-1, keepdims=True)) + norm_eps)
    return (values * inv_rms * gain_vec).astype(jnp.bfloat16)

def rotate(inputs, positions):
    half_dim = HEAD_DIM // 2
    frequency = rope_base ** (-(jnp.arange(half_dim).astype(jnp.float32) * 2.0 / HEAD_DIM))
    angles = positions.astype(jnp.float32)[:, None] * frequency[None, :]
    cosine = jnp.cos(angles)[:, None, :]
    sine_vals = jnp.sin(angles)[:, None, :]
    lower_half = inputs[..., :half_dim]
    upper_half = inputs[..., half_dim:]
    return jnp.concatenate([lower_half * cosine - upper_half * sine_vals, upper_half * cosine + lower_half * sine_vals], axis=-1)

def attend_request(request_item, attn_gain, qkv_weight):
    row_block, page_pool, page_map, length = request_item
    query_width = HEADS * HEAD_DIM
    key_width = KV_HEADS * HEAD_DIM
    group_size = HEADS // KV_HEADS
    attn_in = normalize(row_block, attn_gain)
    projected_all = jnp.dot(attn_in, qkv_weight, preferred_element_type=jnp.float32).astype(jnp.bfloat16)
    positions = length + jnp.arange(NEW).astype(jnp.int32)
    queries = rotate(projected_all[:, :query_width].astype(jnp.float32).reshape(NEW, HEADS, HEAD_DIM), positions).astype(jnp.bfloat16)
    new_keys = rotate(projected_all[:, query_width:query_width + key_width].astype(jnp.float32).reshape(NEW, KV_HEADS, HEAD_DIM), positions).astype(jnp.bfloat16)
    appended = jnp.concatenate([new_keys.reshape(NEW, key_width), projected_all[:, query_width + key_width:]], axis=1)
    page_total = page_map.shape[0]
    page_index = jnp.arange(page_total).astype(jnp.int32)
    logical = lax.optimization_barrier(jnp.sum(jnp.where(page_map[None, :] == page_index[:, None], page_index[None, :], 0), axis=1)).astype(jnp.int32)
    slot_pos = logical[:, None] * PAGE + jnp.arange(PAGE).astype(jnp.int32)[None, :]
    offset = slot_pos - length
    written = (offset >= 0) & (offset < NEW)
    picked = appended[jnp.clip(offset, 0, NEW - 1)]
    pool_out = jnp.where(written[:, :, None], picked, page_pool)
    slot_rows = pool_out.reshape(page_total * PAGE, 2 * key_width)
    key_all = slot_rows[:, :key_width].reshape(-1, KV_HEADS, HEAD_DIM).astype(jnp.float32)
    val_all = slot_rows[:, key_width:].reshape(-1, KV_HEADS, HEAD_DIM).astype(jnp.float32)
    grouped = queries.reshape(NEW, KV_HEADS, group_size, HEAD_DIM).astype(jnp.float32)
    scores = jnp.einsum('tkgd,skd->tkgs', grouped, key_all) * (1.0 / math.sqrt(HEAD_DIM))
    allowed = (slot_pos.reshape(-1)[None, :] <= positions[:, None])[:, None, None, :]
    maxima = lax.optimization_barrier(jnp.max(jnp.where(allowed, scores, -1e+30), axis=-1, keepdims=True))
    weights = jnp.where(allowed, jnp.exp(scores - maxima), 0.0)
    totals = lax.optimization_barrier(jnp.sum(weights, axis=-1))
    probs_low = lax.optimization_barrier(weights.astype(jnp.bfloat16))
    weighted = jnp.einsum('tkgs,skd->tkgd', probs_low.astype(jnp.float32), val_all, precision=lax.Precision.HIGHEST)
    attention = (weighted / totals[..., None]).reshape(NEW, query_width).astype(jnp.bfloat16)
    return (attention, pool_out)

def reference(hidden, attn_gain, qkv_weight, out_weight, kv_pool, page_table, cache_lens, ffn_gain, route_ids, route_weights, shared_gate_up, shared_down, expert_gate_up, expert_down):
    row_blocks = hidden.reshape(REQUESTS, NEW, D)
    attention, pool_out = lax.map(lambda request_item: attend_request(request_item, attn_gain, qkv_weight), (row_blocks, kv_pool, page_table, cache_lens))
    attention = attention.reshape(TOKENS, D)
    mixed_rows = (hidden.astype(jnp.float32) + jnp.dot(attention, out_weight, preferred_element_type=jnp.float32)).astype(jnp.bfloat16)
    ffn_in = normalize(mixed_rows, ffn_gain)
    gate_up = jnp.dot(ffn_in, shared_gate_up.reshape(D, 2 * FF_SHARED), preferred_element_type=jnp.float32)
    shared_act = (jax.nn.silu(gate_up[:, :FF_SHARED]) * gate_up[:, FF_SHARED:]).astype(jnp.bfloat16)
    running_sum = mixed_rows.astype(jnp.float32) + jnp.dot(shared_act, shared_down, preferred_element_type=jnp.float32)
    row_limit = N_EXP * CAP
    token_index = jnp.arange(TOKENS).astype(jnp.int32)

    def one_expert(running, expert):
        route_hits = route_ids == expert
        chosen = jnp.any(route_hits, axis=1)
        weight = lax.optimization_barrier(jnp.sum(jnp.where(route_hits, route_weights, 0.0), axis=1))
        sort_keys = jnp.where(chosen, token_index, TOKENS + token_index).astype(jnp.int32)
        picked_rows = jnp.argsort(sort_keys)[:row_limit].astype(jnp.int32)
        rows_in = ffn_in[picked_rows]
        is_valid = chosen[picked_rows]
        part_weights = lax.dynamic_slice_in_dim(expert_gate_up, expert * SPLIT, SPLIT, 0)
        part_downs = lax.dynamic_slice_in_dim(expert_down, expert * SPLIT, SPLIT, 0)
        summed = jnp.zeros((row_limit, D), jnp.float32)
        for part_index in range(SPLIT):
            expert_gu = jnp.dot(rows_in, part_weights[part_index], preferred_element_type=jnp.float32)
            expert_act = (jax.nn.silu(expert_gu[:, :FF_PART]) * expert_gu[:, FF_PART:]).astype(jnp.bfloat16)
            expert_part = jnp.dot(expert_act, part_downs[part_index], preferred_element_type=jnp.float32).astype(jnp.bfloat16)
            summed = summed + expert_part.astype(jnp.float32)
        contrib = summed * jnp.where(is_valid, weight[picked_rows], 0.0)[:, None]
        return (running.at[picked_rows].add(contrib), None)
    routed, _ = lax.scan(one_expert, jnp.zeros((TOKENS, D), jnp.float32), jnp.arange(EXPERTS).astype(jnp.int32))
    hidden_out = (running_sum + routed).astype(jnp.bfloat16)
    return (hidden_out, pool_out)
```

```python
import functools
import math

import jax
import jax.numpy as jnp
from jax import lax
from jax.experimental import pallas as pl
from jax.experimental.pallas import tpu as pltpu
from jax.sharding import PartitionSpec as P

HEADS = 20
KV_HEADS = 4
HEAD_DIM = 128
TOPK = 6
SPLIT = 4
PAGE = 128
NEW = 256
FF_PART = 384
GROUP = HEADS // KV_HEADS

MESH = pl.DeviceIdType.MESH
VM = pltpu.VMEM
F32 = jnp.float32
BF16 = jnp.bfloat16

rope_base = 500000.0
norm_eps = 1e-05


def remote(src, dst, send, recv, **to):
    return pltpu.make_async_remote_copy(
        src_ref=src, dst_ref=dst, send_sem=send, recv_sem=recv, device_id=to, device_id_type=MESH
    )


def greet(peers):
    barrier = pltpu.get_barrier_semaphore()
    for to in peers:
        pl.semaphore_signal(barrier, inc=1, device_id=to, device_id_type=MESH)
    pl.semaphore_wait(barrier, len(peers))


def place(half):
    me = lax.axis_index("blk")
    chip, core = me // 2, me % 2
    partner = chip * 2 + 1 - core

    def peer(k):
        return ((chip + k + half) % half) * 2 + core

    return me, partner, peer


def gather_kernel(n, x_ref, o_ref, local_sem, send, recv, fsend, frecv):
    half = n // 2
    me, partner, peer = place(half)
    rows = x_ref.shape[0]

    def block(b):
        return o_ref.at[pl.ds(pl.multiple_of(b * rows, 8), rows), :]

    greet([{"blk": peer(k)} for k in range(1, half)] + [{"blk": partner}])
    outs = [remote(x_ref, block(me), send.at[k], recv.at[k], blk=peer(k)) for k in range(1, half)]
    for copy in outs:
        copy.start()
    passed = [remote(x_ref, block(me), fsend.at[0], frecv.at[0], blk=partner)]
    passed[0].start()
    own = pltpu.make_async_copy(x_ref, block(me), local_sem)
    own.start()
    for k in range(1, half):
        outs[k - 1].wait_recv()
        b = peer(-k)
        copy = remote(block(b), block(b), fsend.at[k], frecv.at[k], blk=partner)
        copy.start()
        passed.append(copy)
    for copy in outs:
        copy.wait_send()
    for copy in passed:
        copy.wait()
    own.wait()


def gather_blk(x, collective_id):
    n = lax.axis_size("blk")
    half = n // 2
    dma = pltpu.SemaphoreType.DMA
    return pl.pallas_call(
        functools.partial(gather_kernel, n),
        out_shape=jax.ShapeDtypeStruct((n * x.shape[0], x.shape[1]), x.dtype),
        in_specs=[pl.BlockSpec(memory_space=VM)],
        out_specs=pl.BlockSpec(memory_space=VM),
        scratch_shapes=[dma] + [dma((half,))] * 4,
        compiler_params=pltpu.CompilerParams(
            collective_id=collective_id, has_side_effects=True, vmem_limit_bytes=32 << 20
        ),
        name="gather_blk%d" % collective_id,
    )(x)


def reduce_kernel(n, x_ref, o_ref, r1, s, r2, send1, recv1, send2, recv2):
    half = n // 2
    me, partner, peer = place(half)
    rows = o_ref.shape[0]

    def block(b):
        return pl.ds(pl.multiple_of(b * rows, 16), rows)

    greet([{"blk": peer(k)} for k in range(1, half)] + [{"blk": partner}])
    order = list(range(1, half)) + [0]
    first = {}
    for k in order:
        other = peer(k) + partner - me
        first[k] = remote(x_ref.at[block(other), :], r1.at[k], send1.at[k], recv1.at[k], blk=partner)
        first[k].start()
    second = []
    for k in order:
        first[k].wait_recv()
        s[k] = (x_ref[block(peer(k)), :].astype(F32) + r1[k].astype(F32)).astype(BF16)
        if k:
            copy = remote(s.at[k], r2.at[k], send2.at[k], recv2.at[k], blk=peer(k))
            copy.start()
            second.append(copy)
    total = x_ref[block(me), :].astype(F32) + r1[0].astype(F32)
    for k in range(1, half):
        second[k - 1].wait_recv()
        total += r2[k].astype(F32)
    o_ref[...] = total.astype(o_ref.dtype)
    for k in order:
        first[k].wait_send()
    for copy in second:
        copy.wait_send()


def reduce_blk(x, collective_id):
    n = lax.axis_size("blk")
    half = n // 2
    dma = pltpu.SemaphoreType.DMA
    rows, cols = x.shape[0] // n, x.shape[1]
    return pl.pallas_call(
        functools.partial(reduce_kernel, n),
        out_shape=jax.ShapeDtypeStruct((rows, cols), BF16),
        in_specs=[pl.BlockSpec(memory_space=VM)],
        out_specs=pl.BlockSpec(memory_space=VM),
        scratch_shapes=[VM((half, rows, cols), BF16)] * 3 + [dma((half,))] * 4,
        compiler_params=pltpu.CompilerParams(
            collective_id=collective_id, has_side_effects=True, vmem_limit_bytes=32 << 20
        ),
        name="reduce_blk",
    )(x)


def gather_all_kernel(n, g, x_ref, o_ref, local_sem, zsend, zrecv, bsend, brecv, psend, precv):
    half = n // 2
    me, partner, peer = place(half)
    z = lax.axis_index("exp")
    rows, cols = x_ref.shape

    def zpeer(k):
        return (z + k + g) % g

    def block(b, w):
        return o_ref.at[
            pl.ds(pl.multiple_of(b * rows, 16), rows), pl.ds(pl.multiple_of(w * cols, 128), cols)
        ]

    greet(
        [{"exp": zpeer(k)} for k in range(1, g)]
        + [{"blk": peer(k)} for k in range(1, half)]
        + [{"blk": partner}]
    )
    along = [
        remote(x_ref, block(me, z), zsend.at[k], zrecv.at[k], exp=zpeer(k)) for k in range(1, g)
    ]
    for copy in along:
        copy.start()
    own = pltpu.make_async_copy(x_ref, block(me, z), local_sem)
    own.start()
    outs, passed = {}, []

    def spread(kz):
        w = zpeer(-kz)
        src = x_ref if kz == 0 else block(me, w)
        for k in range(1, half):
            outs[kz, k] = remote(src, block(me, w), bsend.at[kz, k], brecv.at[kz, k], blk=peer(k))
            outs[kz, k].start()
        copy = remote(src, block(me, w), psend.at[kz, 0], precv.at[kz, 0], blk=partner)
        copy.start()
        passed.append(copy)

    def relay(kz):
        w = zpeer(-kz)
        for k in range(1, half):
            outs[kz, k].wait_recv()
            here = block(peer(-k), w)
            copy = remote(here, here, psend.at[kz, k], precv.at[kz, k], blk=partner)
            copy.start()
            passed.append(copy)

    spread(0)
    for kz in range(1, g):
        along[kz - 1].wait_recv()
        spread(kz)
        relay(kz - 1)
    relay(g - 1)
    for copy in along + list(outs.values()):
        copy.wait_send()
    for copy in passed:
        copy.wait()
    own.wait()


def gather_all(x, collective_id):
    n, g = lax.axis_size("blk"), lax.axis_size("exp")
    half = n // 2
    if n * g > 32:
        along = lax.all_gather(x, "exp", axis=1, tiled=True)
        return lax.all_gather(along, "blk", axis=0, tiled=True)
    dma = pltpu.SemaphoreType.DMA
    return pl.pallas_call(
        functools.partial(gather_all_kernel, n, g),
        out_shape=jax.ShapeDtypeStruct((n * x.shape[0], g * x.shape[1]), x.dtype),
        in_specs=[pl.BlockSpec(memory_space=VM)],
        out_specs=pl.BlockSpec(memory_space=VM),
        scratch_shapes=[dma] + [dma((g,))] * 2 + [dma((g, half))] * 4,
        compiler_params=pltpu.CompilerParams(
            collective_id=collective_id, has_side_effects=True, vmem_limit_bytes=40 << 20
        ),
        name="gather_all",
    )(x)


def reduce_all_kernel(
    n, g, x_ref, o_ref, r1, s, r2, t, r3, send1, recv1, send2, recv2, send3, recv3
):
    half = n // 2
    me, partner, peer = place(half)
    z = lax.axis_index("exp")
    rows, cols = o_ref.shape

    def zpeer(k):
        return (z + k + g) % g

    def at(b, w):
        return (
            pl.ds(pl.multiple_of(b * rows, 16), rows),
            pl.ds(pl.multiple_of(w * cols, 128), cols),
        )

    greet(
        [{"exp": zpeer(k)} for k in range(1, g)]
        + [{"blk": peer(k)} for k in range(1, half)]
        + [{"blk": partner}]
    )
    chunks = list(range(1, g)) + [0]
    order = list(range(1, half)) + [0]
    first, second, third = {}, {}, {}
    for kz in chunks:
        for k in order:
            other = peer(k) + partner - me
            first[kz, k] = remote(
                x_ref.at[at(other, zpeer(kz))],
                r1.at[kz, k],
                send1.at[kz, k],
                recv1.at[kz, k],
                blk=partner,
            )
            first[kz, k].start()

    def pair(kz):
        for k in order:
            first[kz, k].wait_recv()
            if k:
                mine = x_ref[at(peer(k), zpeer(kz))].astype(F32)
                s[kz, k] = (mine + r1[kz, k].astype(F32)).astype(BF16)
                second[kz, k] = remote(
                    s.at[kz, k], r2.at[kz, k], send2.at[kz, k], recv2.at[kz, k], blk=peer(k)
                )
                second[kz, k].start()

    def finish(kz):
        total = x_ref[at(me, zpeer(kz))].astype(F32) + r1[kz, 0].astype(F32)
        for k in range(1, half):
            second[kz, k].wait_recv()
            total += r2[kz, k].astype(F32)
        if kz:
            t[kz] = total.astype(BF16)
            third[kz] = remote(t.at[kz], r3.at[kz], send3.at[kz], recv3.at[kz], exp=zpeer(kz))
            third[kz].start()
        return total

    for kz in chunks:
        pair(kz)
    for kz in chunks:
        total = finish(kz)
    for kz in range(1, g):
        third[kz].wait_recv()
        total += r3[kz].astype(F32)
    o_ref[...] = total
    for copy in list(first.values()) + list(second.values()) + list(third.values()):
        copy.wait_send()


def reduce_all(x, collective_id):
    n, g = lax.axis_size("blk"), lax.axis_size("exp")
    half = n // 2
    if n * g > 32:
        part = lax.psum_scatter(x, "blk", scatter_dimension=0, tiled=True)
        return lax.psum_scatter(part, "exp", scatter_dimension=1, tiled=True).astype(F32)
    dma = pltpu.SemaphoreType.DMA
    rows, cols = x.shape[0] // n, x.shape[1] // g
    return pl.pallas_call(
        functools.partial(reduce_all_kernel, n, g),
        out_shape=jax.ShapeDtypeStruct((rows, cols), F32),
        in_specs=[pl.BlockSpec(memory_space=VM)],
        out_specs=pl.BlockSpec(memory_space=VM),
        scratch_shapes=[VM((g, half, rows, cols), BF16)] * 3
        + [VM((g, rows, cols), BF16)] * 2
        + [dma((g, half))] * 4
        + [dma((g,))] * 2,
        compiler_params=pltpu.CompilerParams(
            collective_id=collective_id, has_side_effects=True, vmem_limit_bytes=40 << 20
        ),
        name="reduce_all",
    )(x)


def attend_kernel(q_ref, k_ref, v_ref, kpos_ref, qpos_ref, acc_ref, max_ref, sum_ref):
    allowed = kpos_ref[...] <= qpos_ref[...]
    keys, vals = k_ref[...], v_ref[...]
    for h in range(GROUP):
        scores = jnp.dot(keys, q_ref[h], preferred_element_type=F32) * (1.0 / math.sqrt(HEAD_DIM))
        scores = jnp.where(allowed, scores, -1e30)
        peak = jnp.max(scores, axis=0, keepdims=True)
        weights = jnp.where(allowed, jnp.exp(scores - peak), 0.0)
        max_ref[0, pl.ds(h, 1), :] = peak
        sum_ref[0, pl.ds(h, 1), :] = jnp.sum(weights, axis=0, keepdims=True)
        acc_ref[h] = lax.dot_general(
            vals, weights.astype(BF16), (((0,), (0,)), ((), ())), preferred_element_type=F32
        )


def attend_local(queries, rows, key_pos, query_pos):
    slots = rows.shape[0]
    stat = jax.ShapeDtypeStruct((KV_HEADS, GROUP, NEW), F32)
    return pl.pallas_call(
        attend_kernel,
        grid=(KV_HEADS,),
        out_shape=(jax.ShapeDtypeStruct((HEADS, HEAD_DIM, NEW), F32), stat, stat),
        in_specs=[
            pl.BlockSpec((GROUP, HEAD_DIM, NEW), lambda i: (i, 0, 0)),
            pl.BlockSpec((slots, HEAD_DIM), lambda i: (0, i)),
            pl.BlockSpec((slots, HEAD_DIM), lambda i: (0, i + KV_HEADS)),
            pl.BlockSpec((slots, 1), lambda i: (0, 0)),
            pl.BlockSpec((1, NEW), lambda i: (0, 0)),
        ],
        out_specs=(
            pl.BlockSpec((GROUP, HEAD_DIM, NEW), lambda i: (i, 0, 0)),
            pl.BlockSpec((1, GROUP, NEW), lambda i: (i, 0, 0)),
            pl.BlockSpec((1, GROUP, NEW), lambda i: (i, 0, 0)),
        ),
        compiler_params=pltpu.CompilerParams(vmem_limit_bytes=32 << 20),
        name="attend_local",
    )(queries, rows, rows, key_pos[:, None], query_pos[None, :])


def normalize(inputs, gain_vec):
    values = inputs.astype(F32)
    inv_rms = lax.rsqrt(jnp.mean(values * values, axis=0, keepdims=True) + norm_eps)
    return (values * inv_rms * gain_vec[:, None]).astype(BF16)


def rotate(inputs, positions):
    half_dim = HEAD_DIM // 2
    frequency = rope_base ** (-(jnp.arange(half_dim).astype(F32) * 2.0 / HEAD_DIM))
    angles = frequency[:, None] * positions.astype(F32)[None, :]
    cosine = jnp.cos(angles)[None]
    sine_vals = jnp.sin(angles)[None]
    lower_half = inputs[:, :half_dim]
    upper_half = inputs[:, half_dim:]
    return jnp.concatenate(
        [
            lower_half * cosine - upper_half * sine_vals,
            upper_half * cosine + lower_half * sine_vals,
        ],
        axis=1,
    )


def columns_dot(weight, inputs):
    return lax.dot_general(weight, inputs, (((0,), (0,)), ((), ())), preferred_element_type=F32)


def per_device(
    hidden,
    attn_gain,
    qkv_weight,
    out_weight,
    kv_pool,
    page_table,
    cache_lens,
    ffn_gain,
    route_ids,
    route_weights,
    shared_gate_up,
    shared_down,
    expert_gate_up,
    expert_down,
):
    blocks = lax.axis_size("blk")
    groups = lax.axis_size("exp")
    block_index = lax.axis_index("blk")
    group_index = lax.axis_index("exp")
    model_width = hidden.shape[1] * blocks
    query_width = HEADS * HEAD_DIM
    key_width = KV_HEADS * HEAD_DIM

    expert_count = blocks * groups // SPLIT
    experts = jnp.arange(expert_count, dtype=jnp.int32)
    hits = route_ids.T[None] == experts[:, None, None]
    shares = jnp.sum(jnp.where(hits, route_weights.T[None], 0.0), axis=1)
    all_shares = lax.all_gather(shares, "exp", axis=1, tiled=True)
    own_expert = (block_index * groups + group_index) // SPLIT
    share = lax.dynamic_slice_in_dim(all_shares, own_expert, 1, 0)

    hidden_t = hidden.T
    attn_in = normalize(gather_blk(hidden_t, 1), attn_gain)
    projected = columns_dot(qkv_weight, attn_in).astype(BF16)
    projected_all = gather_blk(projected, 2)
    length = cache_lens[0]
    positions = length + jnp.arange(NEW, dtype=jnp.int32)
    turned = rotate(
        projected_all[: query_width + key_width].astype(F32).reshape(-1, HEAD_DIM, NEW), positions
    ).astype(BF16)
    queries = turned[:HEADS]
    appended = jnp.concatenate(
        [turned[HEADS:].reshape(key_width, NEW), projected_all[query_width + key_width :]], axis=0
    ).T

    page_map = page_table[0]
    pool_pages = page_map.shape[0]
    page_index = jnp.arange(pool_pages, dtype=jnp.int32)
    logical = jnp.sum(
        jnp.where(page_map[None, :] == page_index[:, None], page_index[None, :], 0), axis=1
    )
    local_pages = kv_pool.shape[1]
    local_logical = lax.dynamic_slice_in_dim(logical, block_index * local_pages, local_pages)
    slot_offsets = jnp.arange(PAGE, dtype=jnp.int32)
    local_pos = local_logical[:, None] * PAGE + slot_offsets[None, :]
    offset = local_pos - length
    written = (offset >= 0) & (offset < NEW)
    picked = appended[jnp.clip(offset, 0, NEW - 1)]
    pool_out = jnp.where(written[:, :, None], picked, kv_pool[0])

    acc, peaks, sums = attend_local(
        queries,
        pool_out.reshape(local_pages * PAGE, 2 * key_width),
        local_pos.reshape(-1),
        positions,
    )
    stats = jnp.concatenate([peaks.reshape(HEADS, NEW), sums.reshape(HEADS, NEW)], axis=0)
    all_stats = gather_blk(stats, 3).reshape(blocks, 2, HEADS, NEW)
    top = jnp.max(all_stats[:, 0], axis=0)
    whole = jnp.sum(all_stats[:, 1] * jnp.exp(all_stats[:, 0] - top[None]), axis=0)
    factor = jnp.exp(stats[:HEADS] - top) / whole
    scaled = (acc * factor[:, None, :]).astype(BF16).reshape(query_width, NEW)
    attention = gather_blk(reduce_blk(scaled, 4), 5)
    attended = columns_dot(out_weight, attention)
    mixed = (hidden_t.astype(F32) + attended).astype(BF16)

    ffn_in = normalize(gather_all(mixed, 6), ffn_gain)
    own_in = lax.dynamic_slice_in_dim(ffn_in, group_index * NEW, NEW, 1)
    shared_cols = shared_gate_up.shape[2]
    gate_up = columns_dot(shared_gate_up.reshape(model_width, 2 * shared_cols), own_in)
    shared_act = (jax.nn.silu(gate_up[:shared_cols]) * gate_up[shared_cols:]).astype(BF16)
    shared_term = columns_dot(shared_down, shared_act)

    expert_gu = columns_dot(expert_gate_up[0], ffn_in)
    activated = (jax.nn.silu(expert_gu[:FF_PART]) * expert_gu[FF_PART:]).astype(BF16)
    result = columns_dot(expert_down[0], activated) * share
    mine = (jnp.arange(groups, dtype=jnp.int32) == group_index)[None, :, None]
    layer = result.reshape(model_width, groups, NEW) + jnp.where(mine, shared_term[:, None, :], 0.0)
    summed = reduce_all(layer.astype(BF16).reshape(model_width, groups * NEW), 7)
    hidden_out = (mixed.astype(F32) + summed).astype(BF16)
    return (hidden_out.T, pool_out[None])


def solution(mesh):
    placed = (
        P("exp", "blk"),
        P(),
        P(None, "blk"),
        P(None, "blk"),
        P("exp", "blk", None, None),
        P("exp", None),
        P("exp"),
        P(),
        P("exp", None),
        P("exp", None),
        P(None, None, "blk"),
        P("blk", None),
        P(("blk", "exp"), None, None),
        P(("blk", "exp"), None, None),
    )
    return jax.shard_map(
        per_device,
        mesh=mesh,
        in_specs=placed,
        out_specs=(P("exp", "blk"), P("exp", "blk", None, None)),
        check_vma=False,
    )
```

```python
import functools
import math

import jax
import jax.numpy as jnp
from jax import lax
from jax.experimental import pallas as pl
from jax.experimental.pallas import tpu as pltpu
from jax.sharding import PartitionSpec as P

HEADS = 20
KV_HEADS = 4
HEAD_DIM = 128
TOPK = 6
SPLIT = 4
PAGE = 128
NEW = 256
FF_PART = 384
GROUP = HEADS // KV_HEADS

MESH = pl.DeviceIdType.MESH
VM = pltpu.VMEM
F32 = jnp.float32
BF16 = jnp.bfloat16

rope_base = 500000.0
norm_eps = 1e-05


def remote(src, dst, send, recv, **to):
    return pltpu.make_async_remote_copy(
        src_ref=src, dst_ref=dst, send_sem=send, recv_sem=recv, device_id=to, device_id_type=MESH
    )


def greet(peers):
    barrier = pltpu.get_barrier_semaphore()
    for to in peers:
        pl.semaphore_signal(barrier, inc=1, device_id=to, device_id_type=MESH)
    pl.semaphore_wait(barrier, len(peers))


def place(half):
    me = lax.axis_index("blk")
    chip, core = me // 2, me % 2
    partner = chip * 2 + 1 - core

    def peer(k):
        return ((chip + k + half) % half) * 2 + core

    return me, partner, peer


def gather_kernel(n, x_ref, o_ref, local_sem, send, recv, fsend, frecv):
    half = n // 2
    me, partner, peer = place(half)
    rows = x_ref.shape[0]

    def block(b):
        return o_ref.at[pl.ds(pl.multiple_of(b * rows, 8), rows), :]

    greet([{"blk": peer(k)} for k in range(1, half)] + [{"blk": partner}])
    outs = [remote(x_ref, block(me), send.at[k], recv.at[k], blk=peer(k)) for k in range(1, half)]
    for copy in outs:
        copy.start()
    passed = [remote(x_ref, block(me), fsend.at[0], frecv.at[0], blk=partner)]
    passed[0].start()
    own = pltpu.make_async_copy(x_ref, block(me), local_sem)
    own.start()
    for k in range(1, half):
        outs[k - 1].wait_recv()
        b = peer(-k)
        copy = remote(block(b), block(b), fsend.at[k], frecv.at[k], blk=partner)
        copy.start()
        passed.append(copy)
    for copy in outs:
        copy.wait_send()
    for copy in passed:
        copy.wait()
    own.wait()


def gather_blk(x, collective_id):
    n = lax.axis_size("blk")
    half = n // 2
    dma = pltpu.SemaphoreType.DMA
    return pl.pallas_call(
        functools.partial(gather_kernel, n),
        out_shape=jax.ShapeDtypeStruct((n * x.shape[0], x.shape[1]), x.dtype),
        in_specs=[pl.BlockSpec(memory_space=VM)],
        out_specs=pl.BlockSpec(memory_space=VM),
        scratch_shapes=[dma] + [dma((half,))] * 4,
        compiler_params=pltpu.CompilerParams(
            collective_id=collective_id, has_side_effects=True, vmem_limit_bytes=32 << 20
        ),
        name="gather_blk%d" % collective_id,
    )(x)


def reduce_kernel(n, x_ref, o_ref, r1, s, r2, send1, recv1, send2, recv2):
    half = n // 2
    me, partner, peer = place(half)
    rows = o_ref.shape[0]

    def block(b):
        return pl.ds(pl.multiple_of(b * rows, 16), rows)

    greet([{"blk": peer(k)} for k in range(1, half)] + [{"blk": partner}])
    order = list(range(1, half)) + [0]
    first = {}
    for k in order:
        other = peer(k) + partner - me
        first[k] = remote(x_ref.at[block(other), :], r1.at[k], send1.at[k], recv1.at[k], blk=partner)
        first[k].start()
    second = []
    for k in order:
        first[k].wait_recv()
        s[k] = (x_ref[block(peer(k)), :].astype(F32) + r1[k].astype(F32)).astype(BF16)
        if k:
            copy = remote(s.at[k], r2.at[k], send2.at[k], recv2.at[k], blk=peer(k))
            copy.start()
            second.append(copy)
    total = x_ref[block(me), :].astype(F32) + r1[0].astype(F32)
    for k in range(1, half):
        second[k - 1].wait_recv()
        total += r2[k].astype(F32)
    o_ref[...] = total.astype(o_ref.dtype)
    for k in order:
        first[k].wait_send()
    for copy in second:
        copy.wait_send()


def reduce_blk(x, collective_id):
    n = lax.axis_size("blk")
    half = n // 2
    dma = pltpu.SemaphoreType.DMA
    rows, cols = x.shape[0] // n, x.shape[1]
    return pl.pallas_call(
        functools.partial(reduce_kernel, n),
        out_shape=jax.ShapeDtypeStruct((rows, cols), BF16),
        in_specs=[pl.BlockSpec(memory_space=VM)],
        out_specs=pl.BlockSpec(memory_space=VM),
        scratch_shapes=[VM((half, rows, cols), BF16)] * 3 + [dma((half,))] * 4,
        compiler_params=pltpu.CompilerParams(
            collective_id=collective_id, has_side_effects=True, vmem_limit_bytes=32 << 20
        ),
        name="reduce_blk",
    )(x)


def experts_kernel(
    n, g, eps, x_ref, gain_ref, share_ref, gu_hbm, down_hbm, sgu_hbm, sdown_hbm, o_ref,
    full, part, shares, gu_raw, down_raw, sgu_raw, sdown_raw, gu, down, sgu, sdown,
    normed, hid, act, sact, r1, s, r2, t, r3,
    local_sem, wsem, zsend, zrecv, hsend, hrecv, bsend, brecv, psend, precv,
    send1, recv1, send2, recv2, send3, recv3,
):
    half = n // 2
    me, partner, peer = place(half)
    z = lax.axis_index("exp")
    rows, cols = x_ref.shape
    width, ff = n * rows, act.shape[0]

    def zpeer(k):
        return (z + k + g) % g

    def span(w):
        return pl.ds(pl.multiple_of(w * cols, 128), cols)

    def at(b, w):
        return pl.ds(pl.multiple_of(b * rows, 16), rows), span(w)

    loads = [
        pltpu.make_async_copy(src, dst, wsem.at[i])
        for i, (src, dst) in enumerate(
            [(gu_hbm, gu_raw), (down_hbm, down_raw), (sgu_hbm, sgu_raw), (sdown_hbm, sdown_raw)]
        )
    ]
    for load in loads:
        load.start()
    greet(
        [{"exp": zpeer(k)} for k in range(1, g)]
        + [{"blk": peer(k)} for k in range(1, half)]
        + [{"blk": partner}]
    )
    along = [
        remote(x_ref, full.at[at(me, z)], zsend.at[k], zrecv.at[k], exp=zpeer(k))
        for k in range(1, g)
    ]
    told = [
        remote(share_ref, shares.at[:, span(z)], hsend.at[k], hrecv.at[k], exp=zpeer(k))
        for k in range(1, g)
    ]
    own = pltpu.make_async_copy(x_ref, full.at[at(me, z)], local_sem.at[0])
    own_share = pltpu.make_async_copy(share_ref, shares.at[:, span(z)], local_sem.at[1])
    outs, passed, first, second, third = {}, {}, {}, {}, {}
    order = list(range(1, half)) + [0]

    def spread(kz):
        w = zpeer(-kz)
        if kz:
            along[kz - 1].wait_recv()
        src = x_ref if kz == 0 else full.at[at(me, w)]
        for k in range(1, half):
            outs[kz, k] = remote(
                src, full.at[at(me, w)], bsend.at[kz, k], brecv.at[kz, k], blk=peer(k)
            )
            outs[kz, k].start()
        passed[kz, 0] = remote(
            src, full.at[at(me, w)], psend.at[kz, 0], precv.at[kz, 0], blk=partner
        )
        passed[kz, 0].start()

    def relay(kz):
        w = zpeer(-kz)
        for k in range(1, half):
            outs[kz, k].wait_recv()
            here = full.at[at(peer(-k), w)]
            passed[kz, k] = remote(here, here, psend.at[kz, k], precv.at[kz, k], blk=partner)
            passed[kz, k].start()

    def turn(i, src, dst, step):
        loads[i].wait()

        @pl.loop(0, src.shape[1] // step)
        def _(j):
            c = pl.ds(pl.multiple_of(j * step, 128), step)
            dst[c, :] = src[:, c].T

    def arrive(kz):
        for k in range(half):
            passed[kz, k].wait_recv()

    def norm(kz):
        w = zpeer(-kz)
        tile = 256

        def add(j, total):
            v = full[pl.ds(pl.multiple_of(j * tile, 16), tile), span(w)].astype(F32)
            return total + jnp.sum(v * v, axis=0, keepdims=True)

        total = lax.fori_loop(0, width // tile, add, jnp.zeros((1, cols), F32))
        inv = lax.rsqrt(total * (1.0 / width) + eps)

        @pl.loop(0, width // tile)
        def _(j):
            r = pl.ds(pl.multiple_of(j * tile, 16), tile)
            normed[r, :] = (full[r, span(w)].astype(F32) * inv * gain_ref[r, :]).astype(BF16)

    def hidden_units(weight, out, factor):
        tile = 256

        @pl.loop(0, 2 * ff // tile)
        def _(j):
            r = pl.ds(pl.multiple_of(j * tile, 16), tile)
            hid[r, :] = jnp.dot(weight[r, :], normed[...], preferred_element_type=F32)

        gate = hid[pl.ds(0, ff), :]
        out[...] = (gate / (1.0 + jnp.exp(-gate)) * hid[pl.ds(ff, ff), :] * factor).astype(BF16)

    def expert(kz):
        w = zpeer(-kz)
        row = (me * g + z) // SPLIT
        hidden_units(gu, act, shares[pl.ds(row, 1), span(w)])
        tile = 256

        @pl.loop(0, width // tile)
        def _(j):
            r = pl.ds(pl.multiple_of(j * tile, 16), tile)
            y = jnp.dot(down[r, :], act[...], preferred_element_type=F32)
            if kz == 0:
                y += jnp.dot(sdown[r, :], sact[...], preferred_element_type=F32)
            part[r, span(w)] = y.astype(BF16)

        for k in order:
            other = peer(k) + partner - me
            first[kz, k] = remote(
                part.at[at(other, w)], r1.at[kz, k], send1.at[kz, k], recv1.at[kz, k], blk=partner
            )
            first[kz, k].start()

    def pair(kz):
        for k in order:
            first[kz, k].wait_recv()
            if k:
                mine = part[at(peer(k), zpeer(-kz))].astype(F32)
                s[kz, k] = (mine + r1[kz, k].astype(F32)).astype(BF16)
                second[kz, k] = remote(
                    s.at[kz, k], r2.at[kz, k], send2.at[kz, k], recv2.at[kz, k], blk=peer(k)
                )
                second[kz, k].start()

    def finish(kz):
        total = part[at(me, zpeer(-kz))].astype(F32) + r1[kz, 0].astype(F32)
        for k in range(1, half):
            second[kz, k].wait_recv()
            total += r2[kz, k].astype(F32)
        if kz:
            t[kz] = total.astype(BF16)
            third[kz] = remote(t.at[kz], r3.at[kz], send3.at[kz], recv3.at[kz], exp=zpeer(-kz))
            third[kz].start()
        return total

    spread(0)
    for copy in along + told:
        copy.start()
    own.start()
    own_share.start()
    turn(0, gu_raw, gu, 256)
    spread(1)
    relay(0)
    turn(1, down_raw, down, 512)
    spread(2)
    relay(1)
    own.wait()
    own_share.wait()
    turn(2, sgu_raw, sgu, 256)
    arrive(0)
    spread(3)
    relay(2)
    norm(0)
    hidden_units(sgu, sact, 1.0)
    for copy in told:
        copy.wait()
    arrive(1)
    norm(1)
    expert(1)
    relay(3)
    turn(3, sdown_raw, sdown, 512)
    pair(1)
    arrive(2)
    norm(2)
    expert(2)
    pair(2)
    arrive(3)
    norm(3)
    expert(3)
    pair(3)
    norm(0)
    expert(0)
    pair(0)
    for kz in range(1, g):
        finish(kz)
    total = finish(0)
    for kz in range(1, g):
        third[kz].wait_recv()
        total += r3[kz].astype(F32)
    o_ref[...] = total
    for copy in along + [c for d in (outs, passed, first, second, third) for c in d.values()]:
        copy.wait_send()


def experts_fused(x, gain, share, gate_up, down, shared_gate_up, shared_down, collective_id):
    n, g = lax.axis_size("blk"), lax.axis_size("exp")
    half = n // 2
    dma = pltpu.SemaphoreType.DMA
    rows, cols = x.shape
    width, ff = n * rows, down.shape[0]
    weights = [gate_up, down, shared_gate_up, shared_down]
    return pl.pallas_call(
        functools.partial(experts_kernel, n, g, norm_eps),
        out_shape=jax.ShapeDtypeStruct((rows, cols), F32),
        in_specs=[pl.BlockSpec(memory_space=VM)] * 3 + [pl.BlockSpec(memory_space=pl.ANY)] * 4,
        out_specs=pl.BlockSpec(memory_space=VM),
        scratch_shapes=[VM((width, g * cols), BF16)] * 2
        + [VM((share.shape[0], g * cols), F32)]
        + [VM(w.shape, BF16) for w in weights]
        + [VM(w.shape[::-1], BF16) for w in weights]
        + [VM((width, cols), BF16), VM((2 * ff, cols), F32)]
        + [VM((ff, cols), BF16)] * 2
        + [VM((g, half, rows, cols), BF16)] * 3
        + [VM((g, rows, cols), BF16)] * 2
        + [dma((2,)), dma((4,))]
        + [dma((g,))] * 4
        + [dma((g, half))] * 8
        + [dma((g,))] * 2,
        compiler_params=pltpu.CompilerParams(
            collective_id=collective_id, has_side_effects=True, vmem_limit_bytes=58 << 20
        ),
        name="experts_fused",
    )(x, gain[:, None], share, *weights)


def experts_wide(x, gain, share, gate_up, down, shared_gate_up, shared_down):
    g, z, cols = lax.axis_size("exp"), lax.axis_index("exp"), x.shape[1]
    ff = down.shape[0]
    row = (lax.axis_index("blk") * g + z) // SPLIT
    factor = lax.dynamic_slice_in_dim(lax.all_gather(share, "exp", axis=1, tiled=True), row, 1, 0)
    along = lax.all_gather(x, "exp", axis=1, tiled=True)
    ffn_in = normalize(lax.all_gather(along, "blk", axis=0, tiled=True), gain)
    own_in = lax.dynamic_slice_in_dim(ffn_in, z * cols, cols, 1)
    shared_ff = shared_down.shape[0]
    both = columns_dot(shared_gate_up, own_in)
    shared_act = (jax.nn.silu(both[:shared_ff]) * both[shared_ff:]).astype(BF16)
    gu = columns_dot(gate_up, ffn_in)
    act = (jax.nn.silu(gu[:ff]) * gu[ff:] * factor).astype(BF16)
    layer = columns_dot(down, act)
    own = lax.dynamic_slice_in_dim(layer, z * cols, cols, 1) + columns_dot(shared_down, shared_act)
    layer = lax.dynamic_update_slice_in_dim(layer, own, z * cols, 1).astype(BF16)
    part = lax.psum_scatter(layer, "blk", scatter_dimension=0, tiled=True)
    return lax.psum_scatter(part, "exp", scatter_dimension=1, tiled=True).astype(F32)


def attend_kernel(q_ref, k_ref, v_ref, kpos_ref, qpos_ref, acc_ref, max_ref, sum_ref):
    allowed = kpos_ref[...] <= qpos_ref[...]
    keys, vals = k_ref[...], v_ref[...]
    for h in range(GROUP):
        scores = jnp.dot(keys, q_ref[h], preferred_element_type=F32) * (1.0 / math.sqrt(HEAD_DIM))
        scores = jnp.where(allowed, scores, -1e30)
        peak = jnp.max(scores, axis=0, keepdims=True)
        weights = jnp.where(allowed, jnp.exp(scores - peak), 0.0)
        max_ref[0, pl.ds(h, 1), :] = peak
        sum_ref[0, pl.ds(h, 1), :] = jnp.sum(weights, axis=0, keepdims=True)
        acc_ref[h] = lax.dot_general(
            vals, weights.astype(BF16), (((0,), (0,)), ((), ())), preferred_element_type=F32
        )


def attend_local(queries, rows, key_pos, query_pos):
    slots = rows.shape[0]
    stat = jax.ShapeDtypeStruct((KV_HEADS, GROUP, NEW), F32)
    return pl.pallas_call(
        attend_kernel,
        grid=(KV_HEADS,),
        out_shape=(jax.ShapeDtypeStruct((HEADS, HEAD_DIM, NEW), F32), stat, stat),
        in_specs=[
            pl.BlockSpec((GROUP, HEAD_DIM, NEW), lambda i: (i, 0, 0)),
            pl.BlockSpec((slots, HEAD_DIM), lambda i: (0, i)),
            pl.BlockSpec((slots, HEAD_DIM), lambda i: (0, i + KV_HEADS)),
            pl.BlockSpec((slots, 1), lambda i: (0, 0)),
            pl.BlockSpec((1, NEW), lambda i: (0, 0)),
        ],
        out_specs=(
            pl.BlockSpec((GROUP, HEAD_DIM, NEW), lambda i: (i, 0, 0)),
            pl.BlockSpec((1, GROUP, NEW), lambda i: (i, 0, 0)),
            pl.BlockSpec((1, GROUP, NEW), lambda i: (i, 0, 0)),
        ),
        compiler_params=pltpu.CompilerParams(vmem_limit_bytes=32 << 20),
        name="attend_local",
    )(queries, rows, rows, key_pos[:, None], query_pos[None, :])


def normalize(inputs, gain_vec):
    values = inputs.astype(F32)
    inv_rms = lax.rsqrt(jnp.mean(values * values, axis=0, keepdims=True) + norm_eps)
    return (values * inv_rms * gain_vec[:, None]).astype(BF16)


def rotate(inputs, positions):
    half_dim = HEAD_DIM // 2
    frequency = rope_base ** (-(jnp.arange(half_dim).astype(F32) * 2.0 / HEAD_DIM))
    angles = frequency[:, None] * positions.astype(F32)[None, :]
    cosine = jnp.cos(angles)[None]
    sine_vals = jnp.sin(angles)[None]
    lower_half = inputs[:, :half_dim]
    upper_half = inputs[:, half_dim:]
    return jnp.concatenate(
        [
            lower_half * cosine - upper_half * sine_vals,
            upper_half * cosine + lower_half * sine_vals,
        ],
        axis=1,
    )


def columns_dot(weight, inputs):
    return lax.dot_general(weight, inputs, (((0,), (0,)), ((), ())), preferred_element_type=F32)


def per_device(
    hidden,
    attn_gain,
    qkv_weight,
    out_weight,
    kv_pool,
    page_table,
    cache_lens,
    ffn_gain,
    route_ids,
    route_weights,
    shared_gate_up,
    shared_down,
    expert_gate_up,
    expert_down,
):
    blocks = lax.axis_size("blk")
    groups = lax.axis_size("exp")
    block_index = lax.axis_index("blk")
    model_width = hidden.shape[1] * blocks
    query_width = HEADS * HEAD_DIM
    key_width = KV_HEADS * HEAD_DIM

    expert_count = blocks * groups // SPLIT
    experts = jnp.arange(expert_count, dtype=jnp.int32)
    hits = route_ids.T[None] == experts[:, None, None]
    shares = jnp.sum(jnp.where(hits, route_weights.T[None], 0.0), axis=1)

    hidden_t = hidden.T
    attn_in = normalize(gather_blk(hidden_t, 1), attn_gain)
    projected = columns_dot(qkv_weight, attn_in).astype(BF16)
    projected_all = gather_blk(projected, 2)
    length = cache_lens[0]
    positions = length + jnp.arange(NEW, dtype=jnp.int32)
    turned = rotate(
        projected_all[: query_width + key_width].astype(F32).reshape(-1, HEAD_DIM, NEW), positions
    ).astype(BF16)
    queries = turned[:HEADS]
    appended = jnp.concatenate(
        [turned[HEADS:].reshape(key_width, NEW), projected_all[query_width + key_width :]], axis=0
    ).T

    page_map = page_table[0]
    pool_pages = page_map.shape[0]
    page_index = jnp.arange(pool_pages, dtype=jnp.int32)
    logical = jnp.sum(
        jnp.where(page_map[None, :] == page_index[:, None], page_index[None, :], 0), axis=1
    )
    local_pages = kv_pool.shape[1]
    local_logical = lax.dynamic_slice_in_dim(logical, block_index * local_pages, local_pages)
    slot_offsets = jnp.arange(PAGE, dtype=jnp.int32)
    local_pos = local_logical[:, None] * PAGE + slot_offsets[None, :]
    offset = local_pos - length
    written = (offset >= 0) & (offset < NEW)
    picked = appended[jnp.clip(offset, 0, NEW - 1)]
    pool_out = jnp.where(written[:, :, None], picked, kv_pool[0])

    acc, peaks, sums = attend_local(
        queries,
        pool_out.reshape(local_pages * PAGE, 2 * key_width),
        local_pos.reshape(-1),
        positions,
    )
    stats = jnp.concatenate([peaks.reshape(HEADS, NEW), sums.reshape(HEADS, NEW)], axis=0)
    all_stats = gather_blk(stats, 3).reshape(blocks, 2, HEADS, NEW)
    top = jnp.max(all_stats[:, 0], axis=0)
    whole = jnp.sum(all_stats[:, 1] * jnp.exp(all_stats[:, 0] - top[None]), axis=0)
    factor = jnp.exp(stats[:HEADS] - top) / whole
    scaled = (acc * factor[:, None, :]).astype(BF16).reshape(query_width, NEW)
    attention = gather_blk(reduce_blk(scaled, 4), 5)
    attended = columns_dot(out_weight, attention)
    mixed = (hidden_t.astype(F32) + attended).astype(BF16)

    shared_cols = shared_gate_up.shape[2]
    operands = (
        mixed,
        ffn_gain,
        shares,
        expert_gate_up[0],
        expert_down[0],
        shared_gate_up.reshape(model_width, 2 * shared_cols),
        shared_down,
    )
    if blocks * groups > 32:
        summed = experts_wide(*operands)
    else:
        summed = experts_fused(*operands, 6)
    hidden_out = (mixed.astype(F32) + summed).astype(BF16)
    return (hidden_out.T, pool_out[None])


def solution(mesh):
    placed = (
        P("exp", "blk"),
        P(),
        P(None, "blk"),
        P(None, "blk"),
        P("exp", "blk", None, None),
        P("exp", None),
        P("exp"),
        P(),
        P("exp", None),
        P("exp", None),
        P(None, None, "blk"),
        P("blk", None),
        P(("blk", "exp"), None, None),
        P(("blk", "exp"), None, None),
    )
    return jax.shard_map(
        per_device,
        mesh=mesh,
        in_specs=placed,
        out_specs=(P("exp", "blk"), P("exp", "blk", None, None)),
        check_vma=False,
    )
```

```python
import functools
import math

import jax
import jax.numpy as jnp
from jax import lax
from jax.experimental import pallas as pl
from jax.experimental.pallas import tpu as pltpu
from jax.sharding import PartitionSpec as P

HEADS = 20
KV_HEADS = 4
HEAD_DIM = 128
TOPK = 6
SPLIT = 4
PAGE = 128
NEW = 256
FF_PART = 384
GROUP = HEADS // KV_HEADS

MESH = pl.DeviceIdType.MESH
VM = pltpu.VMEM
F32 = jnp.float32
BF16 = jnp.bfloat16

rope_base = 500000.0
norm_eps = 1e-05


def remote(src, dst, send, recv, **to):
    return pltpu.make_async_remote_copy(
        src_ref=src, dst_ref=dst, send_sem=send, recv_sem=recv, device_id=to, device_id_type=MESH
    )


def greet(peers):
    barrier = pltpu.get_barrier_semaphore()
    for to in peers:
        pl.semaphore_signal(barrier, inc=1, device_id=to, device_id_type=MESH)
    pl.semaphore_wait(barrier, len(peers))


def place(half):
    me = lax.axis_index("blk")
    chip, core = me // 2, me % 2
    partner = chip * 2 + 1 - core

    def peer(k):
        return ((chip + k + half) % half) * 2 + core

    return me, partner, peer


def gather_kernel(n, x_ref, o_ref, local_sem, send, recv, fsend, frecv, meet=True):
    half = n // 2
    me, partner, peer = place(half)
    rows = x_ref.shape[0]

    def block(b):
        return o_ref.at[pl.ds(pl.multiple_of(b * rows, 8), rows), :]

    if meet:
        greet([{"blk": peer(k)} for k in range(1, half)] + [{"blk": partner}])
    outs = [remote(x_ref, block(me), send.at[k], recv.at[k], blk=peer(k)) for k in range(1, half)]
    for copy in outs:
        copy.start()
    passed = [remote(x_ref, block(me), fsend.at[0], frecv.at[0], blk=partner)]
    passed[0].start()
    own = pltpu.make_async_copy(x_ref, block(me), local_sem)
    own.start()
    for k in range(1, half):
        outs[k - 1].wait_recv()
        b = peer(-k)
        copy = remote(block(b), block(b), fsend.at[k], frecv.at[k], blk=partner)
        copy.start()
        passed.append(copy)
    for copy in outs:
        copy.wait_send()
    for copy in passed:
        copy.wait()
    own.wait()


def gather_blk(x, collective_id):
    n = lax.axis_size("blk")
    half = n // 2
    dma = pltpu.SemaphoreType.DMA
    return pl.pallas_call(
        functools.partial(gather_kernel, n),
        out_shape=jax.ShapeDtypeStruct((n * x.shape[0], x.shape[1]), x.dtype),
        in_specs=[pl.BlockSpec(memory_space=VM)],
        out_specs=pl.BlockSpec(memory_space=VM),
        scratch_shapes=[dma] + [dma((half,))] * 4,
        compiler_params=pltpu.CompilerParams(
            collective_id=collective_id, has_side_effects=True, vmem_limit_bytes=32 << 20
        ),
        name="gather_blk%d" % collective_id,
    )(x)


def reduce_kernel(n, x_ref, o_ref, r1, s, r2, send1, recv1, send2, recv2, meet=True):
    half = n // 2
    me, partner, peer = place(half)
    rows = o_ref.shape[0]

    def block(b):
        return pl.ds(pl.multiple_of(b * rows, 16), rows)

    if meet:
        greet([{"blk": peer(k)} for k in range(1, half)] + [{"blk": partner}])
    order = list(range(1, half)) + [0]
    first = {}
    for k in order:
        other = peer(k) + partner - me
        first[k] = remote(x_ref.at[block(other), :], r1.at[k], send1.at[k], recv1.at[k], blk=partner)
        first[k].start()
    second = []
    for k in order:
        first[k].wait_recv()
        s[k] = (x_ref[block(peer(k)), :].astype(F32) + r1[k].astype(F32)).astype(BF16)
        if k:
            copy = remote(s.at[k], r2.at[k], send2.at[k], recv2.at[k], blk=peer(k))
            copy.start()
            second.append(copy)
    total = x_ref[block(me), :].astype(F32) + r1[0].astype(F32)
    for k in range(1, half):
        second[k - 1].wait_recv()
        total += r2[k].astype(F32)
    o_ref[...] = total.astype(o_ref.dtype)
    for k in order:
        first[k].wait_send()
    for copy in second:
        copy.wait_send()


def sum_kernel(n, x_ref, o_ref, own, *scratch):
    reduce_kernel(n, x_ref, own, *scratch[:7])
    gather_kernel(n, own, o_ref, *scratch[7:], meet=False)


def sum_blk(x, collective_id):
    n = lax.axis_size("blk")
    half = n // 2
    dma = pltpu.SemaphoreType.DMA
    rows, cols = x.shape[0] // n, x.shape[1]
    return pl.pallas_call(
        functools.partial(sum_kernel, n),
        out_shape=jax.ShapeDtypeStruct(x.shape, BF16),
        in_specs=[pl.BlockSpec(memory_space=VM)],
        out_specs=pl.BlockSpec(memory_space=VM),
        scratch_shapes=[VM((rows, cols), BF16)]
        + [VM((half, rows, cols), BF16)] * 3
        + [dma((half,))] * 4
        + [dma]
        + [dma((half,))] * 4,
        compiler_params=pltpu.CompilerParams(
            collective_id=collective_id, has_side_effects=True, vmem_limit_bytes=32 << 20
        ),
        name="sum_blk",
    )(x)


def experts_kernel(
    n, g, eps, x_ref, gain_ref, share_ref, gu_hbm, down_hbm, sgu_hbm, sdown_hbm, o_ref,
    full, part, shares, gu_raw, down_raw, sgu_raw, sdown_raw, gu, down, sgu, sdown,
    normed, hid, act, sact, r1, s, r2, t, r3,
    local_sem, wsem, zsend, zrecv, hsend, hrecv, bsend, brecv, psend, precv,
    send1, recv1, send2, recv2, send3, recv3,
):
    half = n // 2
    me, partner, peer = place(half)
    z = lax.axis_index("exp")
    rows, cols = x_ref.shape
    width, ff = n * rows, act.shape[0]

    def zpeer(k):
        return (z + k + g) % g

    def span(w):
        return pl.ds(pl.multiple_of(w * cols, 128), cols)

    def at(b, w):
        return pl.ds(pl.multiple_of(b * rows, 16), rows), span(w)

    loads = [
        pltpu.make_async_copy(src, dst, wsem.at[i])
        for i, (src, dst) in enumerate(
            [(gu_hbm, gu_raw), (down_hbm, down_raw), (sgu_hbm, sgu_raw), (sdown_hbm, sdown_raw)]
        )
    ]
    for load in loads:
        load.start()
    greet(
        [{"exp": zpeer(k)} for k in range(1, g)]
        + [{"blk": peer(k)} for k in range(1, half)]
        + [{"blk": partner}]
    )
    along = [
        remote(x_ref, full.at[at(me, z)], zsend.at[k], zrecv.at[k], exp=zpeer(k))
        for k in range(1, g)
    ]
    told = [
        remote(share_ref, shares.at[:, span(z)], hsend.at[k], hrecv.at[k], exp=zpeer(k))
        for k in range(1, g)
    ]
    own = pltpu.make_async_copy(x_ref, full.at[at(me, z)], local_sem.at[0])
    own_share = pltpu.make_async_copy(share_ref, shares.at[:, span(z)], local_sem.at[1])
    outs, passed, first, second, third = {}, {}, {}, {}, {}
    order = list(range(1, half)) + [0]

    def spread(kz):
        w = zpeer(-kz)
        if kz:
            along[kz - 1].wait_recv()
        src = x_ref if kz == 0 else full.at[at(me, w)]
        for k in range(1, half):
            outs[kz, k] = remote(
                src, full.at[at(me, w)], bsend.at[kz, k], brecv.at[kz, k], blk=peer(k)
            )
            outs[kz, k].start()
        passed[kz, 0] = remote(
            src, full.at[at(me, w)], psend.at[kz, 0], precv.at[kz, 0], blk=partner
        )
        passed[kz, 0].start()

    def relay(kz):
        w = zpeer(-kz)
        for k in range(1, half):
            outs[kz, k].wait_recv()
            here = full.at[at(peer(-k), w)]
            passed[kz, k] = remote(here, here, psend.at[kz, k], precv.at[kz, k], blk=partner)
            passed[kz, k].start()

    def turn(i, src, dst, step):
        loads[i].wait()

        @pl.loop(0, src.shape[1] // step)
        def _(j):
            c = pl.ds(pl.multiple_of(j * step, 128), step)
            dst[c, :] = src[:, c].T

    def arrive(kz):
        for k in range(half):
            passed[kz, k].wait_recv()

    def norm(kz):
        w = zpeer(-kz)
        tile = 256

        def add(j, total):
            v = full[pl.ds(pl.multiple_of(j * tile, 16), tile), span(w)].astype(F32)
            return total + jnp.sum(v * v, axis=0, keepdims=True)

        total = lax.fori_loop(0, width // tile, add, jnp.zeros((1, cols), F32))
        inv = lax.rsqrt(total * (1.0 / width) + eps)

        @pl.loop(0, width // tile)
        def _(j):
            r = pl.ds(pl.multiple_of(j * tile, 16), tile)
            normed[r, :] = (full[r, span(w)].astype(F32) * inv * gain_ref[r, :]).astype(BF16)

    def hidden_units(weight, out, factor):
        tile = 256

        @pl.loop(0, 2 * ff // tile)
        def _(j):
            r = pl.ds(pl.multiple_of(j * tile, 16), tile)
            hid[r, :] = jnp.dot(weight[r, :], normed[...], preferred_element_type=F32)

        gate = hid[pl.ds(0, ff), :]
        out[...] = (gate / (1.0 + jnp.exp(-gate)) * hid[pl.ds(ff, ff), :] * factor).astype(BF16)

    def expert(kz):
        w = zpeer(-kz)
        row = (me * g + z) // SPLIT
        hidden_units(gu, act, shares[pl.ds(row, 1), span(w)])
        tile = 256

        @pl.loop(0, width // tile)
        def _(j):
            r = pl.ds(pl.multiple_of(j * tile, 16), tile)
            y = jnp.dot(down[r, :], act[...], preferred_element_type=F32)
            if kz == 0:
                y += jnp.dot(sdown[r, :], sact[...], preferred_element_type=F32)
            part[r, span(w)] = y.astype(BF16)

        for k in order:
            other = peer(k) + partner - me
            first[kz, k] = remote(
                part.at[at(other, w)], r1.at[kz, k], send1.at[kz, k], recv1.at[kz, k], blk=partner
            )
            first[kz, k].start()

    def pair(kz):
        for k in order:
            first[kz, k].wait_recv()
            if k:
                mine = part[at(peer(k), zpeer(-kz))].astype(F32)
                s[kz, k] = (mine + r1[kz, k].astype(F32)).astype(BF16)
                second[kz, k] = remote(
                    s.at[kz, k], r2.at[kz, k], send2.at[kz, k], recv2.at[kz, k], blk=peer(k)
                )
                second[kz, k].start()

    def finish(kz):
        total = part[at(me, zpeer(-kz))].astype(F32) + r1[kz, 0].astype(F32)
        for k in range(1, half):
            second[kz, k].wait_recv()
            total += r2[kz, k].astype(F32)
        if kz:
            t[kz] = total.astype(BF16)
            third[kz] = remote(t.at[kz], r3.at[kz], send3.at[kz], recv3.at[kz], exp=zpeer(-kz))
            third[kz].start()
        return total

    spread(0)
    for copy in along + told:
        copy.start()
    own.start()
    own_share.start()
    turn(0, gu_raw, gu, 256)
    spread(1)
    relay(0)
    turn(1, down_raw, down, 512)
    spread(2)
    relay(1)
    own.wait()
    own_share.wait()
    turn(2, sgu_raw, sgu, 256)
    arrive(0)
    spread(3)
    relay(2)
    norm(0)
    hidden_units(sgu, sact, 1.0)
    for copy in told:
        copy.wait()
    arrive(1)
    norm(1)
    expert(1)
    relay(3)
    turn(3, sdown_raw, sdown, 512)
    pair(1)
    arrive(2)
    norm(2)
    expert(2)
    pair(2)
    arrive(3)
    norm(3)
    expert(3)
    pair(3)
    norm(0)
    expert(0)
    pair(0)
    for kz in range(1, g):
        finish(kz)
    total = finish(0)
    for kz in range(1, g):
        third[kz].wait_recv()
        total += r3[kz].astype(F32)
    o_ref[...] = total
    for copy in along + [c for d in (outs, passed, first, second, third) for c in d.values()]:
        copy.wait_send()


def experts_fused(x, gain, share, gate_up, down, shared_gate_up, shared_down, collective_id):
    n, g = lax.axis_size("blk"), lax.axis_size("exp")
    half = n // 2
    dma = pltpu.SemaphoreType.DMA
    rows, cols = x.shape
    width, ff = n * rows, down.shape[0]
    weights = [gate_up, down, shared_gate_up, shared_down]
    return pl.pallas_call(
        functools.partial(experts_kernel, n, g, norm_eps),
        out_shape=jax.ShapeDtypeStruct((rows, cols), F32),
        in_specs=[pl.BlockSpec(memory_space=VM)] * 3 + [pl.BlockSpec(memory_space=pl.ANY)] * 4,
        out_specs=pl.BlockSpec(memory_space=VM),
        scratch_shapes=[VM((width, g * cols), BF16)] * 2
        + [VM((share.shape[0], g * cols), F32)]
        + [VM(w.shape, BF16) for w in weights]
        + [VM(w.shape[::-1], BF16) for w in weights]
        + [VM((width, cols), BF16), VM((2 * ff, cols), F32)]
        + [VM((ff, cols), BF16)] * 2
        + [VM((g, half, rows, cols), BF16)] * 3
        + [VM((g, rows, cols), BF16)] * 2
        + [dma((2,)), dma((4,))]
        + [dma((g,))] * 4
        + [dma((g, half))] * 8
        + [dma((g,))] * 2,
        compiler_params=pltpu.CompilerParams(
            collective_id=collective_id, has_side_effects=True, vmem_limit_bytes=58 << 20
        ),
        name="experts_fused",
    )(x, gain[:, None], share, *weights)


def experts_wide(x, gain, share, gate_up, down, shared_gate_up, shared_down):
    g, z, cols = lax.axis_size("exp"), lax.axis_index("exp"), x.shape[1]
    ff = down.shape[0]
    row = (lax.axis_index("blk") * g + z) // SPLIT
    factor = lax.dynamic_slice_in_dim(lax.all_gather(share, "exp", axis=1, tiled=True), row, 1, 0)
    along = lax.all_gather(x, "exp", axis=1, tiled=True)
    ffn_in = normalize(lax.all_gather(along, "blk", axis=0, tiled=True), gain)
    own_in = lax.dynamic_slice_in_dim(ffn_in, z * cols, cols, 1)
    shared_ff = shared_down.shape[0]
    both = columns_dot(shared_gate_up, own_in)
    shared_act = (jax.nn.silu(both[:shared_ff]) * both[shared_ff:]).astype(BF16)
    gu = columns_dot(gate_up, ffn_in)
    act = (jax.nn.silu(gu[:ff]) * gu[ff:] * factor).astype(BF16)
    layer = columns_dot(down, act)
    own = lax.dynamic_slice_in_dim(layer, z * cols, cols, 1) + columns_dot(shared_down, shared_act)
    layer = lax.dynamic_update_slice_in_dim(layer, own, z * cols, 1).astype(BF16)
    part = lax.psum_scatter(layer, "blk", scatter_dimension=0, tiled=True)
    return lax.psum_scatter(part, "exp", scatter_dimension=1, tiled=True).astype(F32)


def attend_kernel(q_ref, k_ref, v_ref, kpos_ref, qpos_ref, acc_ref, max_ref, sum_ref):
    allowed = kpos_ref[...] <= qpos_ref[...]
    keys, vals = k_ref[...], v_ref[...]
    scale = 1.0 / math.sqrt(HEAD_DIM)
    for h in range(GROUP):
        scores = jnp.dot(keys, q_ref[h], preferred_element_type=F32)
        scores = jnp.where(allowed, scores, -1e30)
        peak = jnp.max(scores, axis=0, keepdims=True)
        weights = jnp.exp2((scores - peak) * (scale * math.log2(math.e)))
        max_ref[0, pl.ds(h, 1), :] = peak * scale
        sum_ref[0, pl.ds(h, 1), :] = jnp.sum(weights, axis=0, keepdims=True)
        acc_ref[h] = lax.dot_general(
            vals, weights.astype(BF16), (((0,), (0,)), ((), ())), preferred_element_type=F32
        )


def attend_local(queries, rows, key_pos, query_pos):
    slots = rows.shape[0]
    stat = jax.ShapeDtypeStruct((KV_HEADS, GROUP, NEW), F32)
    return pl.pallas_call(
        attend_kernel,
        grid=(KV_HEADS,),
        out_shape=(jax.ShapeDtypeStruct((HEADS, HEAD_DIM, NEW), F32), stat, stat),
        in_specs=[
            pl.BlockSpec((GROUP, HEAD_DIM, NEW), lambda i: (i, 0, 0)),
            pl.BlockSpec((slots, HEAD_DIM), lambda i: (0, i)),
            pl.BlockSpec((slots, HEAD_DIM), lambda i: (0, i + KV_HEADS)),
            pl.BlockSpec((slots, 1), lambda i: (0, 0)),
            pl.BlockSpec((1, NEW), lambda i: (0, 0)),
        ],
        out_specs=(
            pl.BlockSpec((GROUP, HEAD_DIM, NEW), lambda i: (i, 0, 0)),
            pl.BlockSpec((1, GROUP, NEW), lambda i: (i, 0, 0)),
            pl.BlockSpec((1, GROUP, NEW), lambda i: (i, 0, 0)),
        ),
        compiler_params=pltpu.CompilerParams(vmem_limit_bytes=32 << 20),
        name="attend_local",
    )(queries, rows, rows, key_pos[:, None], query_pos[None, :])


def normalize(inputs, gain_vec):
    values = inputs.astype(F32)
    inv_rms = lax.rsqrt(jnp.mean(values * values, axis=0, keepdims=True) + norm_eps)
    return (values * inv_rms * gain_vec[:, None]).astype(BF16)


def rotate(inputs, positions):
    half_dim = HEAD_DIM // 2
    frequency = rope_base ** (-(jnp.arange(half_dim).astype(F32) * 2.0 / HEAD_DIM))
    angles = frequency[:, None] * positions.astype(F32)[None, :]
    cosine = jnp.cos(angles)[None]
    sine_vals = jnp.sin(angles)[None]
    lower_half = inputs[:, :half_dim]
    upper_half = inputs[:, half_dim:]
    return jnp.concatenate(
        [
            lower_half * cosine - upper_half * sine_vals,
            upper_half * cosine + lower_half * sine_vals,
        ],
        axis=1,
    )


def columns_dot(weight, inputs):
    return lax.dot_general(weight, inputs, (((0,), (0,)), ((), ())), preferred_element_type=F32)


def per_device(
    hidden,
    attn_gain,
    qkv_weight,
    out_weight,
    kv_pool,
    page_table,
    cache_lens,
    ffn_gain,
    route_ids,
    route_weights,
    shared_gate_up,
    shared_down,
    expert_gate_up,
    expert_down,
):
    blocks = lax.axis_size("blk")
    groups = lax.axis_size("exp")
    block_index = lax.axis_index("blk")
    model_width = hidden.shape[1] * blocks
    query_width = HEADS * HEAD_DIM
    key_width = KV_HEADS * HEAD_DIM

    expert_count = blocks * groups // SPLIT
    experts = jnp.arange(expert_count, dtype=jnp.int32)
    hits = route_ids.T[None] == experts[:, None, None]
    shares = jnp.sum(jnp.where(hits, route_weights.T[None], 0.0), axis=1)

    hidden_t = hidden.T
    attn_in = normalize(gather_blk(hidden_t, 1), attn_gain)
    projected = columns_dot(qkv_weight, attn_in).astype(BF16)
    projected_all = gather_blk(projected, 2)
    length = cache_lens[0]
    positions = length + jnp.arange(NEW, dtype=jnp.int32)
    turned = rotate(
        projected_all[: query_width + key_width].astype(F32).reshape(-1, HEAD_DIM, NEW), positions
    ).astype(BF16)
    queries = turned[:HEADS]
    appended = jnp.concatenate(
        [turned[HEADS:].reshape(key_width, NEW), projected_all[query_width + key_width :]], axis=0
    ).T

    page_map = page_table[0]
    pool_pages = page_map.shape[0]
    page_index = jnp.arange(pool_pages, dtype=jnp.int32)
    logical = jnp.sum(
        jnp.where(page_map[None, :] == page_index[:, None], page_index[None, :], 0), axis=1
    )
    local_pages = kv_pool.shape[1]
    local_logical = lax.dynamic_slice_in_dim(logical, block_index * local_pages, local_pages)
    slot_offsets = jnp.arange(PAGE, dtype=jnp.int32)
    local_pos = local_logical[:, None] * PAGE + slot_offsets[None, :]
    offset = local_pos - length
    written = (offset >= 0) & (offset < NEW)
    picked = appended[jnp.clip(offset, 0, NEW - 1)]
    pool_out = jnp.where(written[:, :, None], picked, kv_pool[0])

    acc, peaks, sums = attend_local(
        queries,
        pool_out.reshape(local_pages * PAGE, 2 * key_width),
        local_pos.reshape(-1),
        positions,
    )
    stats = jnp.concatenate([peaks.reshape(HEADS, NEW), sums.reshape(HEADS, NEW)], axis=0)
    all_stats = gather_blk(stats, 3).reshape(blocks, 2, HEADS, NEW)
    top = jnp.max(all_stats[:, 0], axis=0)
    whole = jnp.sum(all_stats[:, 1] * jnp.exp(all_stats[:, 0] - top[None]), axis=0)
    factor = jnp.exp(stats[:HEADS] - top) / whole
    scaled = (acc * factor[:, None, :]).astype(BF16).reshape(query_width, NEW)
    attention = sum_blk(scaled, 4)
    attended = columns_dot(out_weight, attention)
    mixed = (hidden_t.astype(F32) + attended).astype(BF16)

    shared_cols = shared_gate_up.shape[2]
    operands = (
        mixed,
        ffn_gain,
        shares,
        expert_gate_up[0],
        expert_down[0],
        shared_gate_up.reshape(model_width, 2 * shared_cols),
        shared_down,
    )
    if blocks * groups > 32:
        summed = experts_wide(*operands)
    else:
        summed = experts_fused(*operands, 6)
    hidden_out = (mixed.astype(F32) + summed).astype(BF16)
    return (hidden_out.T, pool_out[None])


def solution(mesh):
    placed = (
        P("exp", "blk"),
        P(),
        P(None, "blk"),
        P(None, "blk"),
        P("exp", "blk", None, None),
        P("exp", None),
        P("exp"),
        P(),
        P("exp", None),
        P("exp", None),
        P(None, None, "blk"),
        P("blk", None),
        P(("blk", "exp"), None, None),
        P(("blk", "exp"), None, None),
    )
    return jax.shard_map(
        per_device,
        mesh=mesh,
        in_specs=placed,
        out_specs=(P("exp", "blk"), P("exp", "blk", None, None)),
        check_vma=False,
    )
```

```python
import functools
import math

import jax
import jax.numpy as jnp
from jax import lax
from jax.experimental import pallas as pl
from jax.experimental.pallas import tpu as pltpu
from jax.sharding import PartitionSpec as P

HEADS = 20
KV_HEADS = 4
HEAD_DIM = 128
TOPK = 6
SPLIT = 4
PAGE = 128
NEW = 256
FF_PART = 384
GROUP = HEADS // KV_HEADS

MESH = pl.DeviceIdType.MESH
VM = pltpu.VMEM
F32 = jnp.float32
BF16 = jnp.bfloat16

rope_base = 500000.0
norm_eps = 1e-05


def remote(src, dst, send, recv, **to):
    return pltpu.make_async_remote_copy(
        src_ref=src, dst_ref=dst, send_sem=send, recv_sem=recv, device_id=to, device_id_type=MESH
    )


def greet(peers):
    barrier = pltpu.get_barrier_semaphore()
    for to in peers:
        pl.semaphore_signal(barrier, inc=1, device_id=to, device_id_type=MESH)
    pl.semaphore_wait(barrier, len(peers))


def place(half):
    me = lax.axis_index("blk")
    chip, core = me // 2, me % 2
    partner = chip * 2 + 1 - core

    def peer(k):
        return ((chip + k + half) % half) * 2 + core

    return me, partner, peer


def gather_kernel(n, x_ref, o_ref, local_sem, send, recv, fsend, frecv, meet=True):
    half = n // 2
    me, partner, peer = place(half)
    rows = x_ref.shape[0]

    def block(b):
        return o_ref.at[pl.ds(pl.multiple_of(b * rows, 8), rows), :]

    if meet:
        greet([{"blk": peer(k)} for k in range(1, half)] + [{"blk": partner}])
    outs = [remote(x_ref, block(me), send.at[k], recv.at[k], blk=peer(k)) for k in range(1, half)]
    for copy in outs:
        copy.start()
    passed = [remote(x_ref, block(me), fsend.at[0], frecv.at[0], blk=partner)]
    passed[0].start()
    own = pltpu.make_async_copy(x_ref, block(me), local_sem)
    own.start()
    for k in range(1, half):
        outs[k - 1].wait_recv()
        b = peer(-k)
        copy = remote(block(b), block(b), fsend.at[k], frecv.at[k], blk=partner)
        copy.start()
        passed.append(copy)
    for copy in outs:
        copy.wait_send()
    for copy in passed:
        copy.wait()
    own.wait()


def gather_blk(x, collective_id):
    n = lax.axis_size("blk")
    half = n // 2
    dma = pltpu.SemaphoreType.DMA
    return pl.pallas_call(
        functools.partial(gather_kernel, n),
        out_shape=jax.ShapeDtypeStruct((n * x.shape[0], x.shape[1]), x.dtype),
        in_specs=[pl.BlockSpec(memory_space=VM)],
        out_specs=pl.BlockSpec(memory_space=VM),
        scratch_shapes=[dma] + [dma((half,))] * 4,
        compiler_params=pltpu.CompilerParams(
            collective_id=collective_id, has_side_effects=True, vmem_limit_bytes=32 << 20
        ),
        name="gather_blk%d" % collective_id,
    )(x)


def reduce_kernel(n, x_ref, o_ref, r1, s, r2, send1, recv1, send2, recv2, meet=True):
    half = n // 2
    me, partner, peer = place(half)
    rows = o_ref.shape[0]

    def block(b):
        return pl.ds(pl.multiple_of(b * rows, 16), rows)

    if meet:
        greet([{"blk": peer(k)} for k in range(1, half)] + [{"blk": partner}])
    order = list(range(1, half)) + [0]
    first = {}
    for k in order:
        other = peer(k) + partner - me
        first[k] = remote(x_ref.at[block(other), :], r1.at[k], send1.at[k], recv1.at[k], blk=partner)
        first[k].start()
    second = []
    for k in order:
        first[k].wait_recv()
        s[k] = (x_ref[block(peer(k)), :].astype(F32) + r1[k].astype(F32)).astype(BF16)
        if k:
            copy = remote(s.at[k], r2.at[k], send2.at[k], recv2.at[k], blk=peer(k))
            copy.start()
            second.append(copy)
    total = x_ref[block(me), :].astype(F32) + r1[0].astype(F32)
    for k in range(1, half):
        second[k - 1].wait_recv()
        total += r2[k].astype(F32)
    o_ref[...] = total.astype(o_ref.dtype)
    for k in order:
        first[k].wait_send()
    for copy in second:
        copy.wait_send()


def sum_kernel(n, x_ref, o_ref, own, *scratch):
    reduce_kernel(n, x_ref, own, *scratch[:7])
    gather_kernel(n, own, o_ref, *scratch[7:], meet=False)


def sum_blk(x, collective_id):
    n = lax.axis_size("blk")
    half = n // 2
    dma = pltpu.SemaphoreType.DMA
    rows, cols = x.shape[0] // n, x.shape[1]
    return pl.pallas_call(
        functools.partial(sum_kernel, n),
        out_shape=jax.ShapeDtypeStruct(x.shape, BF16),
        in_specs=[pl.BlockSpec(memory_space=VM)],
        out_specs=pl.BlockSpec(memory_space=VM),
        scratch_shapes=[VM((rows, cols), BF16)]
        + [VM((half, rows, cols), BF16)] * 3
        + [dma((half,))] * 4
        + [dma]
        + [dma((half,))] * 4,
        compiler_params=pltpu.CompilerParams(
            collective_id=collective_id, has_side_effects=True, vmem_limit_bytes=32 << 20
        ),
        name="sum_blk",
    )(x)


def experts_kernel(
    n, g, eps, x_ref, gain_ref, share_ref, gu_hbm, down_hbm, sgu_hbm, sdown_hbm, o_ref,
    full, part, shares, gu_raw, down_raw, sgu_raw, sdown_raw, gu, down, sgu, sdown,
    normed, hid, act, sact, r1, s, r2, t, r3,
    local_sem, wsem, zsend, zrecv, hsend, hrecv, bsend, brecv, psend, precv,
    send1, recv1, send2, recv2, send3, recv3,
):
    half = n // 2
    me, partner, peer = place(half)
    z = lax.axis_index("exp")
    rows, cols = x_ref.shape
    width, ff = n * rows, act.shape[0]

    def zpeer(k):
        return (z + k + g) % g

    def span(w):
        return pl.ds(pl.multiple_of(w * cols, 128), cols)

    def at(b, w):
        return pl.ds(pl.multiple_of(b * rows, 16), rows), span(w)

    loads = [
        pltpu.make_async_copy(src, dst, wsem.at[i])
        for i, (src, dst) in enumerate(
            [(gu_hbm, gu_raw), (down_hbm, down_raw), (sgu_hbm, sgu_raw), (sdown_hbm, sdown_raw)]
        )
    ]
    for load in loads:
        load.start()
    greet(
        [{"exp": zpeer(k)} for k in range(1, g)]
        + [{"blk": peer(k)} for k in range(1, half)]
        + [{"blk": partner}]
    )
    along = [
        remote(x_ref, full.at[at(me, z)], zsend.at[k], zrecv.at[k], exp=zpeer(k))
        for k in range(1, g)
    ]
    told = [
        remote(share_ref, shares.at[:, span(z)], hsend.at[k], hrecv.at[k], exp=zpeer(k))
        for k in range(1, g)
    ]
    own = pltpu.make_async_copy(x_ref, full.at[at(me, z)], local_sem.at[0])
    own_share = pltpu.make_async_copy(share_ref, shares.at[:, span(z)], local_sem.at[1])
    outs, passed, first, second, third = {}, {}, {}, {}, {}
    order = list(range(1, half)) + [0]

    def spread(kz):
        w = zpeer(-kz)
        if kz:
            along[kz - 1].wait_recv()
        src = x_ref if kz == 0 else full.at[at(me, w)]
        for k in range(1, half):
            outs[kz, k] = remote(
                src, full.at[at(me, w)], bsend.at[kz, k], brecv.at[kz, k], blk=peer(k)
            )
            outs[kz, k].start()
        passed[kz, 0] = remote(
            src, full.at[at(me, w)], psend.at[kz, 0], precv.at[kz, 0], blk=partner
        )
        passed[kz, 0].start()

    def relay(kz):
        w = zpeer(-kz)
        for k in range(1, half):
            outs[kz, k].wait_recv()
            here = full.at[at(peer(-k), w)]
            passed[kz, k] = remote(here, here, psend.at[kz, k], precv.at[kz, k], blk=partner)
            passed[kz, k].start()

    def turn(i, src, dst, step):
        loads[i].wait()

        @pl.loop(0, src.shape[1] // step)
        def _(j):
            c = pl.ds(pl.multiple_of(j * step, 128), step)
            dst[c, :] = src[:, c].T

    def arrive(kz):
        for k in range(half):
            passed[kz, k].wait_recv()

    def norm(kz):
        w = zpeer(-kz)
        tile = 256

        def add(j, total):
            v = full[pl.ds(pl.multiple_of(j * tile, 16), tile), span(w)].astype(F32)
            return total + jnp.sum(v * v, axis=0, keepdims=True)

        total = lax.fori_loop(0, width // tile, add, jnp.zeros((1, cols), F32))
        inv = lax.rsqrt(total * (1.0 / width) + eps)

        @pl.loop(0, width // tile)
        def _(j):
            r = pl.ds(pl.multiple_of(j * tile, 16), tile)
            normed[r, :] = (full[r, span(w)].astype(F32) * inv * gain_ref[r, :]).astype(BF16)

    def hidden_units(weight, out, factor):
        tile = 256

        @pl.loop(0, 2 * ff // tile)
        def _(j):
            r = pl.ds(pl.multiple_of(j * tile, 16), tile)
            hid[r, :] = jnp.dot(weight[r, :], normed[...], preferred_element_type=F32)

        gate = hid[pl.ds(0, ff), :]
        out[...] = (gate / (1.0 + jnp.exp(-gate)) * hid[pl.ds(ff, ff), :] * factor).astype(BF16)

    def expert(kz):
        w = zpeer(-kz)
        row = (me * g + z) // SPLIT
        hidden_units(gu, act, shares[pl.ds(row, 1), span(w)])
        tile = 256

        @pl.loop(0, width // tile)
        def _(j):
            r = pl.ds(pl.multiple_of(j * tile, 16), tile)
            y = jnp.dot(down[r, :], act[...], preferred_element_type=F32)
            if kz == 0:
                y += jnp.dot(sdown[r, :], sact[...], preferred_element_type=F32)
            part[r, span(w)] = y.astype(BF16)

        for k in order:
            other = peer(k) + partner - me
            first[kz, k] = remote(
                part.at[at(other, w)], r1.at[kz, k], send1.at[kz, k], recv1.at[kz, k], blk=partner
            )
            first[kz, k].start()

    def pair(kz):
        for k in order:
            first[kz, k].wait_recv()
            if k:
                mine = part[at(peer(k), zpeer(-kz))].astype(F32)
                s[kz, k] = (mine + r1[kz, k].astype(F32)).astype(BF16)
                second[kz, k] = remote(
                    s.at[kz, k], r2.at[kz, k], send2.at[kz, k], recv2.at[kz, k], blk=peer(k)
                )
                second[kz, k].start()

    def finish(kz):
        total = part[at(me, zpeer(-kz))].astype(F32) + r1[kz, 0].astype(F32)
        for k in range(1, half):
            second[kz, k].wait_recv()
            total += r2[kz, k].astype(F32)
        if kz:
            t[kz] = total.astype(BF16)
            third[kz] = remote(t.at[kz], r3.at[kz], send3.at[kz], recv3.at[kz], exp=zpeer(-kz))
            third[kz].start()
        return total

    spread(0)
    for copy in along + told:
        copy.start()
    own.start()
    own_share.start()
    turn(0, gu_raw, gu, 256)
    spread(1)
    relay(0)
    turn(1, down_raw, down, 512)
    spread(2)
    relay(1)
    own.wait()
    own_share.wait()
    turn(2, sgu_raw, sgu, 256)
    arrive(0)
    spread(3)
    relay(2)
    norm(0)
    hidden_units(sgu, sact, 1.0)
    turn(3, sdown_raw, sdown, 512)
    for copy in told:
        copy.wait()
    expert(0)
    arrive(1)
    norm(1)
    expert(1)
    relay(3)
    pair(0)
    pair(1)
    arrive(2)
    norm(2)
    expert(2)
    pair(2)
    arrive(3)
    norm(3)
    expert(3)
    pair(3)
    for kz in range(1, g):
        finish(kz)
    total = finish(0)
    for kz in range(1, g):
        third[kz].wait_recv()
        total += r3[kz].astype(F32)
    o_ref[...] = total
    for copy in along + [c for d in (outs, passed, first, second, third) for c in d.values()]:
        copy.wait_send()


def experts_fused(x, gain, share, gate_up, down, shared_gate_up, shared_down, collective_id):
    n, g = lax.axis_size("blk"), lax.axis_size("exp")
    half = n // 2
    dma = pltpu.SemaphoreType.DMA
    rows, cols = x.shape
    width, ff = n * rows, down.shape[0]
    weights = [gate_up, down, shared_gate_up, shared_down]
    return pl.pallas_call(
        functools.partial(experts_kernel, n, g, norm_eps),
        out_shape=jax.ShapeDtypeStruct((rows, cols), F32),
        in_specs=[pl.BlockSpec(memory_space=VM)] * 3 + [pl.BlockSpec(memory_space=pl.ANY)] * 4,
        out_specs=pl.BlockSpec(memory_space=VM),
        scratch_shapes=[VM((width, g * cols), BF16)] * 2
        + [VM((share.shape[0], g * cols), F32)]
        + [VM(w.shape, BF16) for w in weights]
        + [VM(w.shape[::-1], BF16) for w in weights]
        + [VM((width, cols), BF16), VM((2 * ff, cols), F32)]
        + [VM((ff, cols), BF16)] * 2
        + [VM((g, half, rows, cols), BF16)] * 3
        + [VM((g, rows, cols), BF16)] * 2
        + [dma((2,)), dma((4,))]
        + [dma((g,))] * 4
        + [dma((g, half))] * 8
        + [dma((g,))] * 2,
        compiler_params=pltpu.CompilerParams(
            collective_id=collective_id, has_side_effects=True, vmem_limit_bytes=58 << 20
        ),
        name="experts_fused",
    )(x, gain[:, None], share, *weights)


def experts_wide(x, gain, share, gate_up, down, shared_gate_up, shared_down):
    g, z, cols = lax.axis_size("exp"), lax.axis_index("exp"), x.shape[1]
    ff = down.shape[0]
    row = (lax.axis_index("blk") * g + z) // SPLIT
    factor = lax.dynamic_slice_in_dim(lax.all_gather(share, "exp", axis=1, tiled=True), row, 1, 0)
    along = lax.all_gather(x, "exp", axis=1, tiled=True)
    ffn_in = normalize(lax.all_gather(along, "blk", axis=0, tiled=True), gain)
    own_in = lax.dynamic_slice_in_dim(ffn_in, z * cols, cols, 1)
    shared_ff = shared_down.shape[0]
    both = columns_dot(shared_gate_up, own_in)
    shared_act = (jax.nn.silu(both[:shared_ff]) * both[shared_ff:]).astype(BF16)
    gu = columns_dot(gate_up, ffn_in)
    act = (jax.nn.silu(gu[:ff]) * gu[ff:] * factor).astype(BF16)
    layer = columns_dot(down, act)
    own = lax.dynamic_slice_in_dim(layer, z * cols, cols, 1) + columns_dot(shared_down, shared_act)
    layer = lax.dynamic_update_slice_in_dim(layer, own, z * cols, 1).astype(BF16)
    part = lax.psum_scatter(layer, "blk", scatter_dimension=0, tiled=True)
    return lax.psum_scatter(part, "exp", scatter_dimension=1, tiled=True).astype(F32)


def attend_kernel(q_ref, k_ref, v_ref, kpos_ref, qpos_ref, acc_ref, max_ref, sum_ref):
    allowed = kpos_ref[...] <= qpos_ref[...]
    keys, vals = k_ref[...], v_ref[...]
    scale = 1.0 / math.sqrt(HEAD_DIM)
    for h in range(GROUP):
        scores = jnp.dot(keys, q_ref[h], preferred_element_type=F32)
        scores = jnp.where(allowed, scores, -1e30)
        peak = jnp.max(scores, axis=0, keepdims=True)
        weights = jnp.exp2((scores - peak) * (scale * math.log2(math.e)))
        max_ref[0, pl.ds(h, 1), :] = peak * scale
        sum_ref[0, pl.ds(h, 1), :] = jnp.sum(weights, axis=0, keepdims=True)
        acc_ref[h] = lax.dot_general(
            vals, weights.astype(BF16), (((0,), (0,)), ((), ())), preferred_element_type=F32
        )


def attend_local(queries, rows, key_pos, query_pos):
    slots = rows.shape[0]
    stat = jax.ShapeDtypeStruct((KV_HEADS, GROUP, NEW), F32)
    return pl.pallas_call(
        attend_kernel,
        grid=(KV_HEADS,),
        out_shape=(jax.ShapeDtypeStruct((HEADS, HEAD_DIM, NEW), F32), stat, stat),
        in_specs=[
            pl.BlockSpec((GROUP, HEAD_DIM, NEW), lambda i: (i, 0, 0)),
            pl.BlockSpec((slots, HEAD_DIM), lambda i: (0, i)),
            pl.BlockSpec((slots, HEAD_DIM), lambda i: (0, i + KV_HEADS)),
            pl.BlockSpec((slots, 1), lambda i: (0, 0)),
            pl.BlockSpec((1, NEW), lambda i: (0, 0)),
        ],
        out_specs=(
            pl.BlockSpec((GROUP, HEAD_DIM, NEW), lambda i: (i, 0, 0)),
            pl.BlockSpec((1, GROUP, NEW), lambda i: (i, 0, 0)),
            pl.BlockSpec((1, GROUP, NEW), lambda i: (i, 0, 0)),
        ),
        compiler_params=pltpu.CompilerParams(vmem_limit_bytes=32 << 20),
        name="attend_local",
    )(queries, rows, rows, key_pos[:, None], query_pos[None, :])


def normalize(inputs, gain_vec):
    values = inputs.astype(F32)
    inv_rms = lax.rsqrt(jnp.mean(values * values, axis=0, keepdims=True) + norm_eps)
    return (values * inv_rms * gain_vec[:, None]).astype(BF16)


def rotate(inputs, positions):
    half_dim = HEAD_DIM // 2
    frequency = rope_base ** (-(jnp.arange(half_dim).astype(F32) * 2.0 / HEAD_DIM))
    angles = frequency[:, None] * positions.astype(F32)[None, :]
    cosine = jnp.cos(angles)[None]
    sine_vals = jnp.sin(angles)[None]
    lower_half = inputs[:, :half_dim]
    upper_half = inputs[:, half_dim:]
    return jnp.concatenate(
        [
            lower_half * cosine - upper_half * sine_vals,
            upper_half * cosine + lower_half * sine_vals,
        ],
        axis=1,
    )


def columns_dot(weight, inputs):
    return lax.dot_general(weight, inputs, (((0,), (0,)), ((), ())), preferred_element_type=F32)


def per_device(
    hidden,
    attn_gain,
    qkv_weight,
    out_weight,
    kv_pool,
    page_table,
    cache_lens,
    ffn_gain,
    route_ids,
    route_weights,
    shared_gate_up,
    shared_down,
    expert_gate_up,
    expert_down,
):
    blocks = lax.axis_size("blk")
    groups = lax.axis_size("exp")
    block_index = lax.axis_index("blk")
    model_width = hidden.shape[1] * blocks
    query_width = HEADS * HEAD_DIM
    key_width = KV_HEADS * HEAD_DIM

    expert_count = blocks * groups // SPLIT
    experts = jnp.arange(expert_count, dtype=jnp.int32)
    hits = route_ids.T[None] == experts[:, None, None]
    shares = jnp.sum(jnp.where(hits, route_weights.T[None], 0.0), axis=1)

    hidden_t = hidden.T
    attn_in = normalize(gather_blk(hidden_t, 1), attn_gain)
    projected = columns_dot(qkv_weight, attn_in).astype(BF16)
    projected_all = gather_blk(projected, 2)
    length = cache_lens[0]
    positions = length + jnp.arange(NEW, dtype=jnp.int32)
    turned = rotate(
        projected_all[: query_width + key_width].astype(F32).reshape(-1, HEAD_DIM, NEW), positions
    ).astype(BF16)
    queries = turned[:HEADS]
    appended = jnp.concatenate(
        [turned[HEADS:].reshape(key_width, NEW), projected_all[query_width + key_width :]], axis=0
    ).T

    page_map = page_table[0]
    pool_pages = page_map.shape[0]
    page_index = jnp.arange(pool_pages, dtype=jnp.int32)
    logical = jnp.sum(
        jnp.where(page_map[None, :] == page_index[:, None], page_index[None, :], 0), axis=1
    )
    local_pages = kv_pool.shape[1]
    local_logical = lax.dynamic_slice_in_dim(logical, block_index * local_pages, local_pages)
    slot_offsets = jnp.arange(PAGE, dtype=jnp.int32)
    local_pos = local_logical[:, None] * PAGE + slot_offsets[None, :]
    offset = local_pos - length
    written = (offset >= 0) & (offset < NEW)
    picked = appended[jnp.clip(offset, 0, NEW - 1)]
    pool_out = jnp.where(written[:, :, None], picked, kv_pool[0])

    acc, peaks, sums = attend_local(
        queries,
        pool_out.reshape(local_pages * PAGE, 2 * key_width),
        local_pos.reshape(-1),
        positions,
    )
    stats = jnp.concatenate([peaks.reshape(HEADS, NEW), sums.reshape(HEADS, NEW)], axis=0)
    all_stats = gather_blk(stats, 3).reshape(blocks, 2, HEADS, NEW)
    top = jnp.max(all_stats[:, 0], axis=0)
    whole = jnp.sum(all_stats[:, 1] * jnp.exp(all_stats[:, 0] - top[None]), axis=0)
    factor = jnp.exp(stats[:HEADS] - top) / whole
    scaled = (acc * factor[:, None, :]).astype(BF16).reshape(query_width, NEW)
    attention = sum_blk(scaled, 4)
    attended = columns_dot(out_weight, attention)
    mixed = (hidden_t.astype(F32) + attended).astype(BF16)

    shared_cols = shared_gate_up.shape[2]
    operands = (
        mixed,
        ffn_gain,
        shares,
        expert_gate_up[0],
        expert_down[0],
        shared_gate_up.reshape(model_width, 2 * shared_cols),
        shared_down,
    )
    if blocks * groups > 32:
        summed = experts_wide(*operands)
    else:
        summed = experts_fused(*operands, 6)
    hidden_out = (mixed.astype(F32) + summed).astype(BF16)
    return (hidden_out.T, pool_out[None])


def solution(mesh):
    placed = (
        P("exp", "blk"),
        P(),
        P(None, "blk"),
        P(None, "blk"),
        P("exp", "blk", None, None),
        P("exp", None),
        P("exp"),
        P(),
        P("exp", None),
        P("exp", None),
        P(None, None, "blk"),
        P("blk", None),
        P(("blk", "exp"), None, None),
        P(("blk", "exp"), None, None),
    )
    return jax.shard_map(
        per_device,
        mesh=mesh,
        in_specs=placed,
        out_specs=(P("exp", "blk"), P("exp", "blk", None, None)),
        check_vma=False,
    )
```
